512 devices in a mesh: dp: 32 (over y, z_hi), seq: 16 (over z_lo, x, core).
Axes of the slice: x: 4, y: 8, z: 8 (z_hi: 4, z_lo: 2; z = z_hi * 2 + z_lo), core: 2. Of those that a mesh axis runs over, the one named last changes fastest.
Arguments:
- clips: bfloat16 [32, 16, 128, 1152], P('dp', 'seq'), may hold values from -6 to 6
- qkv_spatial: bfloat16 [3, 1152, 576], P(None, 'dp'), may hold values from -16 to 16
- out_spatial: bfloat16 [576, 1152], P('dp'), may hold values from -0.25 to 0.25
- qkv_temporal: bfloat16 [3, 1152, 576], P(None, 'dp'), may hold values from -16 to 16
- out_temporal: bfloat16 [576, 1152], P('dp'), may hold values from -0.25 to 0.25
- cotangent: bfloat16 [32, 16, 128, 1152], P('dp', 'seq'), may hold values from -6 to 6
Outputs:
- mixed_out: bfloat16 [32, 16, 128, 1152], P('dp', 'seq')
- input_grad: bfloat16 [32, 16, 128, 1152], P('dp', 'seq')
- out_temporal_grad: float32 [576, 1152], P('dp')
The draws below stay inside these ranges and needn't reach their ends.
All inputs are finite; a program needn't handle non-finite values.
Results may differ from the reference program's by a relative error of at most 0.034.
Values may be sent and summed in bfloat16 or wider, within the bound.
No kernel may reach another device: no remote copies, remote signals or barrier semaphores. Data moves between devices by JAX's collectives and lax.ppermute only.
A program may use at most 64 MiB of HBM per device.

```python
import jax
import jax.numpy as jnp
from jax import lax

D = 1152
HEADS = 8
HEAD_DIM = 72
PATCHES = 128
FRAMES = 16
CLIPS = 32


def qkv_law(key, strength):
    first, second = jax.random.split(key)
    width = HEADS * HEAD_DIM
    base = jnp.clip(jax.random.normal(first, (3, D, width), jnp.float32), -4.0, 4.0) * D ** (-0.5)
    levels = strength * (0.5 + jax.random.uniform(second, (HEADS,), jnp.float32))
    per_column = jnp.repeat(levels, HEAD_DIM)
    key_part = base[1] + per_column[None, :] * base[0]
    return jnp.stack([base[0], key_part, base[2]]).astype(jnp.bfloat16)


def draw_qkv_spatial(key, part):
    key = jax.random.fold_in(key, 11)
    strength = 0.0
    return qkv_law(key, strength)


def draw_qkv_temporal(key, part):
    key = jax.random.fold_in(key, 23)
    strength = 0.0
    return qkv_law(key, strength)


def shard_levels(rng, dims, cuts, low, top_value):
    def one(axis_at, parts):
        heights = jax.random.uniform(jax.random.fold_in(jax.random.fold_in(rng, 6), axis_at), (parts,), jnp.float32, low / len(cuts), top_value / len(cuts))
        return jnp.repeat(jnp.exp(heights), dims[axis_at] // parts).reshape((-1,) + (1,) * (len(dims) - axis_at - 1))

    gain = one(*cuts[0])
    for cut in cuts[1:]:
        gain = gain * one(*cut)
    return gain


def gaussian(key, extent, deviation, most, pieces=(), held_as=jnp.bfloat16):
    drawn = jax.random.normal(key, extent, jnp.float32) * deviation
    if len(pieces) > 0:
        drawn = shard_levels(key, extent, pieces, -0.22, 0.18) * drawn
    return jnp.clip(drawn, min=-most, max=most).astype(held_as)


def setup_inputs(seed: int = 0) -> dict:
    key_of = jax.random.split(jax.random.key(seed), 7)
    return {
        "clips": gaussian(key_of[0], (CLIPS, FRAMES, PATCHES, D), 1.0, 6.0, ((0, 32), (1, 16))),
        "qkv_spatial": draw_qkv_spatial(jax.random.fold_in(key_of[6], 71), 0),
        "out_spatial": gaussian(key_of[2], (HEADS * HEAD_DIM, D), (HEADS * HEAD_DIM) ** -0.5, 0.25, ((0, 32),)),
        "qkv_temporal": draw_qkv_temporal(jax.random.fold_in(key_of[6], 71), 0),
        "out_temporal": gaussian(key_of[4], (HEADS * HEAD_DIM, D), (HEADS * HEAD_DIM) ** -0.5, 0.25, ((0, 32),)),
        "cotangent": gaussian(key_of[5], (CLIPS, FRAMES, PATCHES, D), 1.0, 6.0, ((0, 32), (1, 16))),
    }


EPSILON = 1e-06

def normalize(values):
    centred = values - lax.optimization_barrier(jnp.mean(values, axis=-1, keepdims=True))
    inverse = lax.rsqrt(lax.optimization_barrier(jnp.mean(centred * centred, axis=-1, keepdims=True)) + EPSILON)
    return (centred * inverse, inverse)

def norm_back(grad, normed, inverse):
    return inverse * (grad - lax.optimization_barrier(jnp.mean(grad, axis=-1, keepdims=True)) - normed * lax.optimization_barrier(jnp.mean(grad * normed, axis=-1, keepdims=True)))

def attend(queries, key_rows, value_rows, layout):
    key_layout = layout.replace('l', 'm')
    scaling = queries.shape[-1] ** (-0.5)
    scores = jnp.einsum(layout + ',' + key_layout + '->bhlm', queries.astype(jnp.float32), key_rows.astype(jnp.float32)) * scaling
    scores = scores - lax.optimization_barrier(jnp.max(scores, axis=-1, keepdims=True))
    powers = jnp.exp(scores)
    softmax_out = powers / lax.optimization_barrier(jnp.sum(powers, axis=-1, keepdims=True))
    rounded = softmax_out.astype(jnp.bfloat16).astype(jnp.float32)
    context = jnp.einsum('bhlm,' + key_layout + '->' + layout, rounded, value_rows.astype(jnp.float32))
    return (context.astype(jnp.bfloat16), softmax_out)

def attend_back(queries, key_rows, value_rows, softmax_out, context, context_grad, layout):
    key_layout = layout.replace('l', 'm')
    scaling = queries.shape[-1] ** (-0.5)
    rounded = softmax_out.astype(jnp.bfloat16).astype(jnp.float32)
    grad_f = context_grad.astype(jnp.float32)
    value_grad = jnp.einsum('bhlm,' + layout + '->' + key_layout, rounded, grad_f).astype(jnp.bfloat16)
    prob_grad = jnp.einsum(layout + ',' + key_layout + '->bhlm', grad_f, value_rows.astype(jnp.float32))
    row_dots = jnp.einsum(layout + ',' + layout + '->bhl', grad_f, context.astype(jnp.float32))
    score_grad = (softmax_out * (prob_grad - row_dots[..., None]) * scaling).astype(jnp.bfloat16).astype(jnp.float32)
    query_grad = jnp.einsum('bhlm,' + key_layout + '->' + layout, score_grad, key_rows.astype(jnp.float32)).astype(jnp.bfloat16)
    key_grad = jnp.einsum('bhlm,' + layout + '->' + key_layout, score_grad, queries.astype(jnp.float32)).astype(jnp.bfloat16)
    return jnp.stack([query_grad, key_grad, value_grad])

def project(normed, weight):
    return jnp.einsum('fpd,tdc->tfpc', normed.astype(jnp.float32), weight.astype(jnp.float32)).astype(jnp.bfloat16)

def back_project(grads, weight):
    return jnp.einsum('tfpc,tdc->fpd', grads.astype(jnp.float32), weight.astype(jnp.float32))

def reference(clips, qkv_spatial, out_spatial, qkv_temporal, out_temporal, cotangent):
    width = HEADS * HEAD_DIM

    def one_clip(total, pair):
        inputs, out_grad = pair
        frame_count, patch_count = (inputs.shape[0], inputs.shape[1])
        inputs_f = inputs.astype(jnp.float32)
        normed_s, inverse_s = normalize(inputs_f)
        heads_s = project(normed_s.astype(jnp.bfloat16), qkv_spatial).reshape(3, frame_count, patch_count, HEADS, HEAD_DIM)
        context_s, probs_s = attend(heads_s[0], heads_s[1], heads_s[2], 'blhe')
        flat_s = context_s.reshape(frame_count, patch_count, width)
        hidden = (inputs_f + jnp.einsum('fpc,cd->fpd', flat_s.astype(jnp.float32), out_spatial.astype(jnp.float32))).astype(jnp.bfloat16)
        hidden_f = hidden.astype(jnp.float32)
        normed_t, inverse_t = normalize(hidden_f)
        heads_t = project(normed_t.astype(jnp.bfloat16), qkv_temporal).reshape(3, frame_count, patch_count, HEADS, HEAD_DIM)
        context_t, probs_t = attend(heads_t[0], heads_t[1], heads_t[2], 'lbhe')
        flat_t = context_t.reshape(frame_count, patch_count, width)
        mixed = (hidden_f + jnp.einsum('fpc,cd->fpd', flat_t.astype(jnp.float32), out_temporal.astype(jnp.float32))).astype(jnp.bfloat16)
        weight_grad = jnp.dot(flat_t.reshape(-1, width).T, out_grad.reshape(-1, out_grad.shape[-1]), preferred_element_type=jnp.float32)
        out_grad_f = out_grad.astype(jnp.float32)
        grad_t = jnp.einsum('fpd,cd->fpc', out_grad_f, out_temporal.astype(jnp.float32)).astype(jnp.bfloat16)
        grads_t = attend_back(heads_t[0], heads_t[1], heads_t[2], probs_t, context_t, grad_t.reshape(frame_count, patch_count, HEADS, HEAD_DIM), 'lbhe')
        normal_grad_b = back_project(grads_t.reshape(3, frame_count, patch_count, width), qkv_temporal).astype(jnp.bfloat16)
        normal_grad_t = lax.optimization_barrier(normal_grad_b).astype(jnp.float32)
        hidden_grad = (out_grad_f + norm_back(normal_grad_t, normed_t, inverse_t)).astype(jnp.bfloat16)
        hidden_grad_f = hidden_grad.astype(jnp.float32)
        grad_s = jnp.einsum('fpd,cd->fpc', hidden_grad_f, out_spatial.astype(jnp.float32)).astype(jnp.bfloat16)
        grads_s = attend_back(heads_s[0], heads_s[1], heads_s[2], probs_s, context_s, grad_s.reshape(frame_count, patch_count, HEADS, HEAD_DIM), 'blhe')
        normal_grad_s = back_project(grads_s.reshape(3, frame_count, patch_count, width), qkv_spatial)
        input_grad = (hidden_grad_f + norm_back(normal_grad_s, normed_s, inverse_s)).astype(jnp.bfloat16)
        return (total + weight_grad, (mixed, input_grad))
    start = jnp.zeros((width, clips.shape[-1]), jnp.float32)
    weight_grad, (mixed_out, input_grad) = lax.scan(one_clip, start, (clips, cotangent))
    return (mixed_out, input_grad, weight_grad)
```

```python
import functools

import jax
import jax.numpy as jnp
from jax import lax
from jax.experimental import pallas as pl
from jax.experimental.pallas import tpu as pltpu
from jax.sharding import PartitionSpec as P

BF = jnp.bfloat16
F32 = jnp.float32
EPSILON = 1e-06
D = 1152
WIDTH = 576
PAD = 640
HEADS = 8
HEAD = 72
TOKENS = 128
PATCH_BLOCK = 8
SCALING = HEAD ** (-0.5)
SHARE = 288
QK, V_ROWS, O_ROWS, ALL_ROWS = 0, 1152, 1728, 2304
VMEM_LIMIT = 48 * 1024 * 1024


def nn(a, b):
    return lax.dot_general(a, b, (((1,), (0,)), ((), ())), preferred_element_type=F32)


def nt(a, b):
    return lax.dot_general(a, b, (((1,), (1,)), ((), ())), preferred_element_type=F32)


def tn(a, b):
    return lax.dot_general(a, b, (((0,), (0,)), ((), ())), preferred_element_type=F32)


def lanes(shape):
    return lax.broadcasted_iota(jnp.int32, shape, len(shape) - 1)


def normalize(values):
    centred = values - jnp.mean(values, axis=-1, keepdims=True)
    inverse = lax.rsqrt(jnp.mean(centred * centred, axis=-1, keepdims=True) + EPSILON)
    return centred * inverse, inverse


def norm_back(grad, normed, inverse):
    return inverse * (
        grad
        - jnp.mean(grad, axis=-1, keepdims=True)
        - normed * jnp.mean(grad * normed, axis=-1, keepdims=True)
    )


def keep_width(a):
    return jnp.where(lanes(a.shape) < WIDTH, a, 0.0)


def window(h):
    low = h * HEAD // 128 * 128
    high = -(-(h * HEAD + HEAD) // 128) * 128
    return low, high


def head_mask(h):
    low, high = window(h)
    at = lanes((TOKENS, high - low)) + low
    return (at >= h * HEAD) & (at < h * HEAD + HEAD)


def add_window(tiles, h, part):
    low, high = window(h)
    part = jnp.where(head_mask(h), part, 0.0)
    for t in range(low // 128, high // 128):
        piece = part[:, t * 128 - low : t * 128 - low + 128]
        tiles[t] = piece if tiles[t] is None else tiles[t] + piece


def join(tiles):
    return jnp.concatenate(tiles, axis=1)


def project(normed, weights):
    normed_b = normed.astype(BF)
    qk = nn(normed_b, weights[QK:V_ROWS, :])
    swapped = pltpu.roll(normed, WIDTH, 1)
    first = keep_width(normed[:, :PAD]).astype(BF)
    second = keep_width(swapped[:, :PAD]).astype(BF)
    v = nn(first, weights[V_ROWS : V_ROWS + PAD, :PAD])
    v = v + pltpu.roll(nn(second, weights[V_ROWS : V_ROWS + PAD, D - PAD :]), WIDTH, 1)
    k = pltpu.roll(qk, WIDTH, 1)
    return qk[:, :PAD].astype(BF), k[:, :PAD].astype(BF), keep_width(v).astype(BF)


def back_project(dq, dk, dv, weights):
    zeros = jnp.zeros((TOKENS, D - PAD), F32)
    dqk = jnp.concatenate([dq, zeros], axis=1) + pltpu.roll(
        jnp.concatenate([dk, zeros], axis=1), WIDTH, 1
    )
    grad = nt(dqk.astype(BF), weights[QK:V_ROWS, :])
    first = nt(dv.astype(BF), weights[V_ROWS : V_ROWS + PAD, :PAD])
    second = nt(pltpu.roll(dv, PAD - WIDTH, 1).astype(BF), weights[V_ROWS : V_ROWS + PAD, D - PAD :])
    first = jnp.concatenate([keep_width(first), zeros], axis=1)
    second = jnp.concatenate([keep_width(second), zeros], axis=1)
    return grad + first + pltpu.roll(second, WIDTH, 1)


def rounded(a):
    return a.astype(BF).astype(F32)


def attend(q, k, v, allowed, probs_ref):
    tiles = [None] * (PAD // 128)
    for h in range(HEADS):
        low, high = window(h)
        masked = jnp.where(head_mask(h), q[:, low:high].astype(F32), 0.0).astype(BF)
        scores = nt(masked, k[:, low:high]) * SCALING
        if allowed is not None:
            scores = jnp.where(allowed, scores, -1e38)
        powers = jnp.exp(scores - jnp.max(scores, axis=-1, keepdims=True))
        probs = powers / jnp.sum(powers, axis=-1, keepdims=True)
        probs_ref[h] = probs
        add_window(tiles, h, nn(probs.astype(BF), v[:, low:high]))
    return join(tiles).astype(BF)


def attend_back(q, k, v, context, context_grad, probs_ref):
    dq, dk, dv = ([None] * (PAD // 128) for _ in range(3))
    for h in range(HEADS):
        low, high = window(h)
        grad = context_grad[:, low:high]
        masked = jnp.where(head_mask(h), grad.astype(F32), 0.0)
        probs = probs_ref[h]
        prob_grad = nt(masked.astype(BF), v[:, low:high])
        row = jnp.sum(masked * context[:, low:high].astype(F32), axis=-1, keepdims=True)
        score_grad = (probs * (prob_grad - row) * SCALING).astype(BF)
        add_window(dv, h, tn(probs.astype(BF), grad))
        add_window(dq, h, nn(score_grad, k[:, low:high]))
        add_window(dk, h, tn(score_grad, q[:, low:high]))
    return rounded(join(dq)), rounded(join(dk)), rounded(join(dv))


def load_weights(core_ref, own_ref, other_ref, weights, sems):
    core = core_ref[0]
    copies = []
    for half, ref in ((core, own_ref), (1 - core, other_ref)):
        for i in range(8):
            at = pl.multiple_of(i * SHARE + half * (SHARE // 2), SHARE // 2)
            copies.append(
                pltpu.make_async_copy(
                    ref.at[i], weights.at[pl.ds(at, SHARE // 2), :], sems.at[len(copies)]
                )
            )
    for copy in copies:
        copy.start()
    for copy in copies:
        copy.wait()


def prepare_kernel(x_ref, cot_ref, order_ref, x_out, cot_out, normed_out):
    order = order_ref[...]
    x = nn(x_ref[...], order)
    x_out[...] = x.astype(BF)
    cot_out[...] = nn(cot_ref[...], order).astype(BF)
    normed_out[...] = normalize(x)[0]


def forward_kernel(
    core_ref, x_ref, normed_ref, own_ref, other_ref, order_ref, hidden_ref, qkv_ref, probs_ref,
    context_ref, weights, sems,
):
    load_weights(core_ref, own_ref, other_ref, weights, sems)
    q, k, v = project(normed_ref[...], weights)
    qkv_ref[0], qkv_ref[1], qkv_ref[2] = q, k, v
    context = attend(q, k, v, None, probs_ref)
    context_ref[...] = context
    ordered = nn(context, order_ref[...]).astype(BF)
    out = nn(ordered, weights[ALL_ROWS - PAD :, :])
    hidden_ref[...] = (x_ref[...].astype(F32) + out).astype(BF)


def temporal_kernel(
    core_ref, hidden_ref, cot_ref, own_ref, other_ref, order_ref, mixed_ref, grad_ref, share_ref,
    weights, probs, sems,
):
    load_weights(core_ref, own_ref, other_ref, weights, sems)
    hidden = hidden_ref[...].astype(F32)
    normed, inverse = normalize(hidden)
    q, k, v = project(rounded(normed), weights)
    rows = lax.broadcasted_iota(jnp.int32, (TOKENS, TOKENS), 0)
    cols = lax.broadcasted_iota(jnp.int32, (TOKENS, TOKENS), 1)
    allowed = (rows & (PATCH_BLOCK - 1)) == (cols & (PATCH_BLOCK - 1))
    context = attend(q, k, v, allowed, probs)
    order = order_ref[...]
    ordered = nn(context, order).astype(BF)
    out_weights = weights[ALL_ROWS - PAD :, :]
    mixed_ref[...] = (hidden + nn(ordered, out_weights)).astype(BF)
    cot = cot_ref[...]
    share_ref[...] = tn(ordered, cot)[PAD - WIDTH :, :].astype(BF)
    context_grad = nt(nt(cot, out_weights).astype(BF), order).astype(BF)
    dq, dk, dv = attend_back(q, k, v, context, context_grad, probs)
    normed_grad = rounded(back_project(dq, dk, dv, weights))
    grad_ref[...] = (cot.astype(F32) + norm_back(normed_grad, normed, inverse)).astype(BF)


def backward_kernel(
    core_ref, x_ref, grad_ref, mixed_ref, qkv_ref, probs_ref, context_ref, own_ref, other_ref,
    order_ref, full_ref, input_grad_ref, mixed_out, weights, sems,
):
    load_weights(core_ref, own_ref, other_ref, weights, sems)
    full = full_ref[...]
    mixed_out[...] = nt(mixed_ref[...], full).astype(BF)
    grad = grad_ref[...]
    context_grad = nt(nt(grad, weights[ALL_ROWS - PAD :, :]).astype(BF), order_ref[...]).astype(BF)
    dq, dk, dv = attend_back(
        qkv_ref[0], qkv_ref[1], qkv_ref[2], context_ref[...], context_grad, probs_ref
    )
    normed_grad = back_project(dq, dk, dv, weights)
    normed, inverse = normalize(x_ref[...].astype(F32))
    total = grad.astype(F32) + norm_back(normed_grad, normed, inverse)
    input_grad_ref[...] = nt(total.astype(BF), full).astype(BF)


def call(kernel, outs, scratch, flops, *args, smem=True, hbm=()):
    in_specs = []
    for at in range(len(args)):
        space = pltpu.VMEM
        if smem and at == 0:
            space = pltpu.SMEM
        elif at in hbm:
            space = pl.ANY
        in_specs.append(pl.BlockSpec(memory_space=space))
    return pl.pallas_call(
        kernel,
        out_shape=[jax.ShapeDtypeStruct(s, t) for s, t in outs],
        in_specs=in_specs,
        out_specs=[pl.BlockSpec(memory_space=pltpu.VMEM) for _ in outs],
        scratch_shapes=scratch,
        compiler_params=pltpu.CompilerParams(vmem_limit_bytes=VMEM_LIMIT),
        cost_estimate=pl.CostEstimate(flops=flops, bytes_accessed=10_000_000, transcendentals=0),
    )(*args)


def place_in_share(dp, row):
    y, z = dp // 4, dp % 4
    return (z // 2) * 144 + y * 18 + (z % 2) * 9 + row


def model_order():
    n = jnp.arange(D)
    dp, row = n // 36, n % 36
    at = (row // 9) * SHARE + place_in_share(dp, row % 9)
    return (at[:, None] == jnp.arange(D)[None, :]).astype(BF)


def context_order():
    f = jnp.arange(PAD)
    dp, row = f // 18, f % 18
    at = PAD - WIDTH + (row // 9) * SHARE + place_in_share(dp, row % 9)
    at = jnp.where(f < WIDTH, at, -1)
    return (at[:, None] == jnp.arange(PAD)[None, :]).astype(BF)


def order_columns(a):
    rows = a.shape[0]
    a = a.reshape(rows, 8, 2, 2, 4, 9)
    return a.transpose(0, 4, 2, 1, 3, 5).reshape(rows, D)


def restore_columns(a):
    rows = a.shape[0]
    a = a.reshape(rows, 4, 2, 8, 2, 9)
    return a.transpose(0, 3, 2, 4, 1, 5).reshape(rows, D)


GROUPS_Z = [[y * 4 + z for z in range(4)] for y in range(8)]
GROUPS_Y = [[y * 4 + z for y in range(8)] for z in range(4)]
GROUPS_CHIP = [[2 * i + c for i in range(8)] for c in range(2)]
SWAP = [(s, s ^ 1) for s in range(16)]


def spread(block, axis, groups):
    count = len(groups[0])
    return lax.all_to_all(
        jnp.broadcast_to(block[None], (count,) + block.shape), axis, 0, 0,
        axis_index_groups=groups, tiled=True,
    )


def local_rows(qkv, out):
    q, k, v = qkv[0], qkv[1], qkv[2]
    return jnp.concatenate(
        [
            jnp.concatenate([q, k], axis=1),
            jnp.concatenate([v[:18], v[18:]], axis=1),
            order_columns(out),
        ],
        axis=0,
    )


def per_device(clips, qkv_spatial, out_spatial, qkv_temporal, out_temporal, cotangent):
    x = clips.reshape(TOKENS, D)
    out_grad = cotangent.reshape(TOKENS, D)
    seq = lax.axis_index("seq")
    chip, core = seq // 2, seq % 2
    core_arg = core.reshape(1).astype(jnp.int32)

    rows = jnp.stack([local_rows(qkv_spatial, out_spatial), local_rows(qkv_temporal, out_temporal)])
    mine = lax.dynamic_slice_in_dim(rows, chip * 9, 9, axis=1)
    four = spread(mine, "dp", GROUPS_Z).reshape(4, 2, 9, D)
    half = lax.dynamic_slice_in_dim(four, core * 2, 2, axis=0)
    half = half.transpose(1, 0, 2, 3).reshape(36, D)
    column = spread(half, "dp", GROUPS_Y).reshape(8, 2, 18, D)
    blocks = column.transpose(1, 0, 2, 3).reshape(2, 144, D)
    own_s = spread(blocks[0], "seq", GROUPS_CHIP).reshape(8, 144, D)
    other_s = lax.ppermute(own_s, "seq", SWAP)
    own_t = spread(blocks[1], "seq", GROUPS_CHIP).reshape(8, 144, D)
    other_t = lax.ppermute(own_t, "seq", SWAP)

    full_order = model_order()
    small_order = context_order()
    tokens_b = ((TOKENS, D), BF)
    tokens_f = ((TOKENS, D), F32)
    weights = pltpu.VMEM((ALL_ROWS, D), BF)
    sems = pltpu.SemaphoreType.DMA((16,))
    probs = (HEADS, TOKENS, TOKENS)

    x_o, cot_o, normed = call(
        prepare_kernel, [tokens_b, tokens_b, tokens_f], [], 700_000_000, x, out_grad, full_order, smem=False
    )

    def to_patches(a):
        return lax.all_to_all(a.reshape(16, PATCH_BLOCK, D), "seq", 0, 0, tiled=True).reshape(
            TOKENS, D
        )

    cot_p = to_patches(cot_o)
    hidden, qkv, probs_s, context_s = call(
        forward_kernel,
        [tokens_b, ((3, TOKENS, PAD), BF), (probs, F32), ((TOKENS, PAD), BF)],
        [weights, sems],
        700_000_000,
        core_arg, x_o, normed, own_s, other_s, small_order,
        hbm=(3, 4),
    )
    hidden_p = to_patches(hidden)
    mixed_p, grad_p, share = call(
        temporal_kernel,
        [tokens_b, tokens_b, ((WIDTH, D), BF)],
        [weights, pltpu.VMEM(probs, F32), sems],
        1_600_000_000,
        core_arg, hidden_p, cot_p, own_t, other_t, small_order,
        hbm=(3, 4),
    )
    back = lax.all_to_all(
        jnp.concatenate([grad_p, mixed_p], axis=1).reshape(16, PATCH_BLOCK, 2 * D),
        "seq", 0, 0, tiled=True,
    ).reshape(TOKENS, 2 * D)
    input_grad, mixed = call(
        backward_kernel,
        [tokens_b, tokens_b],
        [weights, sems],
        800_000_000,
        core_arg, x_o, back[:, :D], back[:, D:], qkv, probs_s, context_s, own_s, other_s,
        small_order, full_order,
        hbm=(7, 8),
    )

    share = share.reshape(2, SHARE, D)
    keep = lax.dynamic_index_in_dim(share, core, 0, keepdims=False)
    send = lax.dynamic_index_in_dim(share, 1 - core, 0, keepdims=False)
    both = (keep.astype(F32) + lax.ppermute(send, "seq", SWAP).astype(F32)).astype(BF)
    both = both.reshape(2, 8, 2, 9, D).transpose(1, 0, 2, 3, 4).reshape(8, 36, D)
    over_y = lax.all_to_all(both, "dp", 0, 0, axis_index_groups=GROUPS_Y, tiled=True)
    over_y = jnp.sum(over_y.astype(F32), axis=0).astype(BF).reshape(4, 9, D)
    over_z = lax.all_to_all(over_y, "dp", 0, 0, axis_index_groups=GROUPS_Z, tiled=True)
    over_z = jnp.sum(over_z.astype(F32), axis=0).astype(BF)
    over_seq = spread(over_z, "seq", [list(range(16))]).reshape(8, 2, 9, D)
    out_temporal_grad = restore_columns(jnp.sum(over_seq.astype(F32), axis=0).reshape(18, D))

    return mixed[None, None], input_grad[None, None], out_temporal_grad


def solution(mesh):
    tokens = P("dp", "seq", None, None)
    placed = (tokens, P(None, "dp", None), P("dp", None), P(None, "dp", None), P("dp", None), tokens)
    return jax.shard_map(
        per_device,
        mesh=mesh,
        in_specs=placed,
        out_specs=(tokens, tokens, P("dp", None)),
        check_vma=False,
    )
```

```python
import functools

import jax
import jax.numpy as jnp
from jax import lax
from jax.experimental import pallas as pl
from jax.experimental.pallas import tpu as pltpu
from jax.sharding import PartitionSpec as P

BF = jnp.bfloat16
F32 = jnp.float32
EPSILON = 1e-06
D = 1152
WIDTH = 576
PAD = 640
HEADS = 8
HEAD = 72
TOKENS = 128
PATCH_BLOCK = 8
SCALING = HEAD ** (-0.5)
SHARE = 288
QK, V_ROWS, O_ROWS, ALL_ROWS = 0, 1152, 1728, 2304
VMEM_LIMIT = 48 * 1024 * 1024
RING = (0, 1, -1, 2, -2, 3, -3, 4)


def nn(a, b):
    return lax.dot_general(a, b, (((1,), (0,)), ((), ())), preferred_element_type=F32)


def nt(a, b):
    return lax.dot_general(a, b, (((1,), (1,)), ((), ())), preferred_element_type=F32)


def tn(a, b):
    return lax.dot_general(a, b, (((0,), (0,)), ((), ())), preferred_element_type=F32)


def lanes(shape):
    return lax.broadcasted_iota(jnp.int32, shape, len(shape) - 1)


def normalize(values):
    centred = values - jnp.mean(values, axis=-1, keepdims=True)
    inverse = lax.rsqrt(jnp.mean(centred * centred, axis=-1, keepdims=True) + EPSILON)
    return centred * inverse, inverse


def norm_back(grad, normed, inverse):
    return inverse * (
        grad
        - jnp.mean(grad, axis=-1, keepdims=True)
        - normed * jnp.mean(grad * normed, axis=-1, keepdims=True)
    )


def keep_width(a):
    return jnp.where(lanes(a.shape) < WIDTH, a, 0.0)


def window(h):
    low = h * HEAD // 128 * 128
    high = -(-(h * HEAD + HEAD) // 128) * 128
    return low, high


def head_mask(h):
    low, high = window(h)
    at = lanes((TOKENS, high - low)) + low
    return (at >= h * HEAD) & (at < h * HEAD + HEAD)


def add_window(tiles, h, part):
    low, high = window(h)
    part = jnp.where(head_mask(h), part, 0.0)
    for t in range(low // 128, high // 128):
        piece = part[:, t * 128 - low : t * 128 - low + 128]
        tiles[t] = piece if tiles[t] is None else tiles[t] + piece


def join(tiles):
    return jnp.concatenate(tiles, axis=1)


def project(normed, weights):
    normed_b = normed.astype(BF)
    qk = nn(normed_b, weights[QK:V_ROWS, :])
    swapped = pltpu.roll(normed, WIDTH, 1)
    first = keep_width(normed[:, :PAD]).astype(BF)
    second = keep_width(swapped[:, :PAD]).astype(BF)
    v = nn(first, weights[V_ROWS : V_ROWS + PAD, :PAD])
    v = v + pltpu.roll(nn(second, weights[V_ROWS : V_ROWS + PAD, D - PAD :]), WIDTH, 1)
    k = pltpu.roll(qk, WIDTH, 1)
    return qk[:, :PAD].astype(BF), k[:, :PAD].astype(BF), keep_width(v).astype(BF)


def back_project(dq, dk, dv, weights):
    zeros = jnp.zeros((TOKENS, D - PAD), F32)
    dqk = jnp.concatenate([dq, zeros], axis=1) + pltpu.roll(
        jnp.concatenate([dk, zeros], axis=1), WIDTH, 1
    )
    grad = nt(dqk.astype(BF), weights[QK:V_ROWS, :])
    first = nt(dv.astype(BF), weights[V_ROWS : V_ROWS + PAD, :PAD])
    second = nt(pltpu.roll(dv, PAD - WIDTH, 1).astype(BF), weights[V_ROWS : V_ROWS + PAD, D - PAD :])
    first = jnp.concatenate([keep_width(first), zeros], axis=1)
    second = jnp.concatenate([keep_width(second), zeros], axis=1)
    return grad + first + pltpu.roll(second, WIDTH, 1)


def rounded(a):
    return a.astype(BF).astype(F32)


def attend(q, k, v, allowed, probs_ref):
    tiles = [None] * (PAD // 128)
    for h in range(HEADS):
        low, high = window(h)
        masked = jnp.where(head_mask(h), q[:, low:high].astype(F32), 0.0).astype(BF)
        scores = nt(masked, k[:, low:high]) * SCALING
        if allowed is not None:
            scores = jnp.where(allowed, scores, -1e38)
        powers = jnp.exp(scores - jnp.max(scores, axis=-1, keepdims=True))
        probs = powers / jnp.sum(powers, axis=-1, keepdims=True)
        probs_ref[h] = probs
        add_window(tiles, h, nn(probs.astype(BF), v[:, low:high]))
    return join(tiles).astype(BF)


def attend_back(q, k, v, context, context_grad, probs_ref):
    dq, dk, dv = ([None] * (PAD // 128) for _ in range(3))
    for h in range(HEADS):
        low, high = window(h)
        grad = context_grad[:, low:high]
        masked = jnp.where(head_mask(h), grad.astype(F32), 0.0)
        probs = probs_ref[h]
        prob_grad = nt(masked.astype(BF), v[:, low:high])
        row = jnp.sum(masked * context[:, low:high].astype(F32), axis=-1, keepdims=True)
        score_grad = (probs * (prob_grad - row) * SCALING).astype(BF)
        add_window(dv, h, tn(probs.astype(BF), grad))
        add_window(dq, h, nn(score_grad, k[:, low:high]))
        add_window(dk, h, tn(score_grad, q[:, low:high]))
    return rounded(join(dq)), rounded(join(dk)), rounded(join(dv))


def start_all(copies):
    for copy in copies:
        copy.start()
    for copy in copies:
        copy.wait()


def load_spatial(at_ref, blocks, swapped, weights, sems):
    y, core = at_ref[0], at_ref[1]
    copies = []
    for half, mine in ((core, True), (1 - core, False)):
        sign = 1 - 2 * half
        for n, step in enumerate(RING):
            source = blocks[n] if mine else swapped[n // 4].at[n % 4]
            place = lax.rem(y - sign * step + 16, 8)
            at = pl.multiple_of(half * D + place * 144, 144)
            copies.append(
                pltpu.make_async_copy(
                    source, weights.at[pl.ds(at, 144), :], sems.at[len(copies)]
                )
            )
    start_all(copies)


def load_temporal(at_ref, own_ref, other_ref, weights, sems):
    core = at_ref[1]
    copies = []
    for half, ref in ((core, own_ref), (1 - core, other_ref)):
        for i in range(8):
            at = pl.multiple_of(i * SHARE + half * (SHARE // 2), SHARE // 2)
            copies.append(
                pltpu.make_async_copy(
                    ref.at[i], weights.at[pl.ds(at, SHARE // 2), :], sems.at[len(copies)]
                )
            )
    start_all(copies)


def project_spatial(normed, weights):
    normed_b = normed.astype(BF)
    qk = nn(normed_b, weights[:D, :])
    v = keep_width(nn(normed_b, weights[D:, :PAD]))
    k = pltpu.roll(qk, WIDTH, 1)
    return qk[:, :PAD].astype(BF), k[:, :PAD].astype(BF), v.astype(BF)


def pair_lanes(dq, dk):
    zeros = jnp.zeros((TOKENS, D - PAD), F32)
    return jnp.concatenate([dq, zeros], axis=1) + pltpu.roll(
        jnp.concatenate([dk, zeros], axis=1), WIDTH, 1
    )


def back_project_spatial(dq, dk, dv, weights):
    return nt(pair_lanes(dq, dk).astype(BF), weights[:D, :]) + nt(
        dv.astype(BF), weights[D:, :PAD]
    )


def late(a):
    return jnp.where(lanes(a.shape) >= PAD - WIDTH, a, 0.0)


def out_spatial_of(context, expand, weights):
    zeros = jnp.zeros((TOKENS, D - PAD), F32)
    spread_out = nn(context, expand)
    first = late(nn(spread_out.astype(BF), weights[D:, D - PAD :]))
    second = late(nn(pltpu.roll(spread_out, 18, 1).astype(BF), weights[D:, D - PAD :]))
    return pltpu.roll(
        jnp.concatenate([first, zeros], axis=1), D - (PAD - WIDTH), 1
    ) + jnp.concatenate([zeros, second], axis=1)


def context_grad_spatial(grad, expand, weights):
    first = late(pltpu.roll(grad, PAD - WIDTH, 1)[:, :PAD])
    second = late(grad[:, D - PAD :])
    total = nt(first.astype(BF), weights[D:, D - PAD :]) + pltpu.roll(
        nt(second.astype(BF), weights[D:, D - PAD :]), D - 18, 1
    )
    return nt(total.astype(BF), expand).astype(BF)


def selection(rows, columns, shift):
    r = lax.broadcasted_iota(jnp.int32, (rows, columns), 0)
    c = lax.broadcasted_iota(jnp.int32, (rows, columns), 1)
    return r + shift == c


def pack_kernel(at_ref, qkv_s, out_s, qkv_t, out_t, block_ref):
    chip, core = at_ref[2], at_ref[1]

    def pick(which, a):
        return nn(which.astype(F32).astype(BF), a)

    def side(a, b):
        return jnp.concatenate([a, b], axis=1)

    def rows(count, at, size):
        return selection(count, size, at)

    q, k, v, out = qkv_s[0], qkv_s[1], qkv_s[2], out_s[...]
    lead = selection(36, 18, 0)
    tail = selection(36, 18, -18)
    halves = pick(lead, out[:, :WIDTH]) + pick(tail, out[:, WIDTH:])
    first = side(q.astype(F32), k.astype(F32))
    second = side(v.astype(F32), halves)
    spatial = jnp.where(core == 0, first, second)

    q, k, v, out = qkv_t[0], qkv_t[1], qkv_t[2], out_t[...]
    nine = lax.broadcasted_iota(jnp.int32, (12, 1), 0) < 9

    def inside(low, high):
        return nine & (chip >= low) & (chip < high)

    here = rows(12, chip * 9, 36) & inside(0, 4)
    upper = rows(12, (chip - 4) * 9, 36) & inside(4, 6)
    lower = rows(12, (chip - 4) * 9 + 18, 36) & inside(4, 6)
    last = rows(12, (chip - 6) * 9, 18) & inside(6, 8)
    temporal = side(pick(here, q) + pick(upper, v), pick(here, k) + pick(lower, v))
    temporal = temporal + pick(last, out)
    block = jnp.concatenate([spatial, temporal], axis=0).astype(BF)
    for z in range(4):
        block_ref[z] = block


def forward_kernel(*refs):
    (at_ref, x_ref, expand_ref), refs = refs[:3], refs[3:]
    blocks, swapped, refs = refs[:8], refs[8:10], refs[10:]
    hidden_ref, qkv_ref, probs_ref, context_ref, weights, sems = refs
    load_spatial(at_ref, blocks, swapped, weights, sems)
    x = x_ref[...].astype(F32)
    q, k, v = project_spatial(normalize(x)[0], weights)
    qkv_ref[0], qkv_ref[1], qkv_ref[2] = q, k, v
    context = attend(q, k, v, None, probs_ref)
    context_ref[...] = context
    hidden_ref[...] = (x + out_spatial_of(context, expand_ref[...], weights)).astype(BF)


def temporal_kernel(
    at_ref, hidden_ref, cot_ref, own_ref, other_ref, order_ref, full_ref, mixed_ref, grad_ref,
    share_ref, weights, probs, sems,
):
    load_temporal(at_ref, own_ref, other_ref, weights, sems)
    hidden = hidden_ref[...].astype(F32)
    full = full_ref[...]
    normed, inverse = normalize(hidden)
    q, k, v = project(nn(normed.astype(BF), full), weights)
    rows = lax.broadcasted_iota(jnp.int32, (TOKENS, TOKENS), 0)
    cols = lax.broadcasted_iota(jnp.int32, (TOKENS, TOKENS), 1)
    allowed = (rows & (PATCH_BLOCK - 1)) == (cols & (PATCH_BLOCK - 1))
    context = attend(q, k, v, allowed, probs)
    order = order_ref[...]
    ordered = nn(context, order).astype(BF)
    out_weights = weights[ALL_ROWS - PAD :, :]
    mixed_ref[...] = (hidden + nn(ordered, out_weights)).astype(BF)
    cot = cot_ref[...]
    share_ref[...] = tn(ordered, cot)[PAD - WIDTH :, :].astype(BF)
    context_grad = nt(nt(cot, out_weights).astype(BF), order).astype(BF)
    dq, dk, dv = attend_back(q, k, v, context, context_grad, probs)
    normed_grad = nt(back_project(dq, dk, dv, weights).astype(BF), full)
    grad_ref[...] = (cot.astype(F32) + norm_back(normed_grad, normed, inverse)).astype(BF)


def backward_kernel(*refs):
    (at_ref, x_ref, grad_ref, qkv_ref, probs_ref, context_ref, expand_ref), refs = refs[:7], refs[7:]
    blocks, swapped, refs = refs[:8], refs[8:10], refs[10:]
    input_grad_ref, weights, sems = refs
    load_spatial(at_ref, blocks, swapped, weights, sems)
    grad = grad_ref[...].astype(F32)
    context_grad = context_grad_spatial(grad, expand_ref[...], weights)
    dq, dk, dv = attend_back(
        qkv_ref[0], qkv_ref[1], qkv_ref[2], context_ref[...], context_grad, probs_ref
    )
    normed_grad = back_project_spatial(dq, dk, dv, weights)
    normed, inverse = normalize(x_ref[...].astype(F32))
    input_grad_ref[...] = (grad + norm_back(normed_grad, normed, inverse)).astype(BF)


def call(kernel, outs, scratch, flops, *args, smem=True, hbm=()):
    in_specs = []
    for at in range(len(args)):
        space = pltpu.VMEM
        if smem and at == 0:
            space = pltpu.SMEM
        elif at in hbm:
            space = pl.ANY
        in_specs.append(pl.BlockSpec(memory_space=space))
    return pl.pallas_call(
        kernel,
        out_shape=[jax.ShapeDtypeStruct(s, t) for s, t in outs],
        in_specs=in_specs,
        out_specs=[pl.BlockSpec(memory_space=pltpu.VMEM) for _ in outs],
        scratch_shapes=scratch,
        compiler_params=pltpu.CompilerParams(vmem_limit_bytes=VMEM_LIMIT),
        cost_estimate=pl.CostEstimate(flops=flops, bytes_accessed=10_000_000, transcendentals=0),
    )(*args)


def place_in_share(dp, row):
    y, z = dp // 4, dp % 4
    return (z // 2) * 144 + y * 18 + (z % 2) * 9 + row


def model_order():
    n = jnp.arange(D)
    dp, row = n // 36, n % 36
    at = (row // 9) * SHARE + place_in_share(dp, row % 9)
    return (at[:, None] == jnp.arange(D)[None, :]).astype(BF)


def context_order():
    f = jnp.arange(PAD)
    dp, row = f // 18, f % 18
    at = PAD - WIDTH + (row // 9) * SHARE + place_in_share(dp, row % 9)
    at = jnp.where(f < WIDTH, at, -1)
    return (at[:, None] == jnp.arange(PAD)[None, :]).astype(BF)


def expand_order():
    f = jnp.arange(PAD)
    at = jnp.where(f < WIDTH, 36 * (f // 18) + f % 18, -1)
    return (at[:, None] == jnp.arange(D)[None, :]).astype(BF)


GROUPS_Z = [[y * 4 + z for z in range(4)] for y in range(8)]
GROUPS_Y = [[y * 4 + z for y in range(8)] for z in range(4)]
GROUPS_CHIP = [[2 * i + c for i in range(8)] for c in range(2)]
SWAP = [(s, s ^ 1) for s in range(16)]


def spread(block, axis, groups):
    count = len(groups[0])
    return lax.all_to_all(
        jnp.broadcast_to(block[None], (count,) + block.shape), axis, 0, 0,
        axis_index_groups=groups, tiled=True,
    )


def along_y(distance):
    pairs = []
    for y in range(8):
        for z in range(4):
            for s in range(16):
                to = (y + (distance if s % 2 == 0 else -distance)) % 8
                pairs.append(((y * 4 + z) * 16 + s, (to * 4 + z) * 16 + s))
    return pairs


UP, DOWN = along_y(1), along_y(-1)


def move(a, pairs):
    return lax.ppermute(a, ("dp", "seq"), pairs)


def per_device(clips, qkv_spatial, out_spatial, qkv_temporal, out_temporal, cotangent):
    x = clips.reshape(TOKENS, D)
    out_grad = cotangent.reshape(TOKENS, D)
    seq, dp = lax.axis_index("seq"), lax.axis_index("dp")
    y, chip, core = dp // 4, seq // 2, seq % 2
    at = jnp.stack([y, core, chip]).astype(jnp.int32)

    tokens_b = ((TOKENS, D), BF)
    probs = (HEADS, TOKENS, TOKENS)
    sems = pltpu.SemaphoreType.DMA((16,))

    def to_patches(a):
        return lax.all_to_all(a.reshape(16, PATCH_BLOCK, D), "seq", 0, 0, tiled=True).reshape(
            TOKENS, D
        )

    (packed,) = call(
        pack_kernel, [((4, 48, D), BF)], [], 100_000_000, at, qkv_spatial, out_spatial,
        qkv_temporal, out_temporal,
    )
    four = lax.all_to_all(packed, "dp", 0, 0, axis_index_groups=GROUPS_Z, tiled=True)
    block = four[:, :36].reshape(144, D)
    column = lax.dynamic_slice_in_dim(four, core * 2, 2, axis=0)[:, 36:45].reshape(1, 18, D)

    up, down = [block], [block]
    up.append(move(block, UP))
    down.append(move(block, DOWN))
    column = jnp.concatenate([column, move(column, along_y(4))])
    up.append(move(up[-1], UP))
    down.append(move(down[-1], DOWN))
    column = jnp.concatenate([column, move(column, along_y(-2))])
    up.append(move(up[-1], UP))
    down.append(move(down[-1], DOWN))
    column = jnp.concatenate([column, move(column, along_y(-1))])
    up.append(move(up[-1], UP))
    blocks = [block, up[1], down[1], up[2], down[2], up[3], down[3], up[4]]
    swapped = [lax.ppermute(jnp.stack(blocks[n : n + 4]), "seq", SWAP) for n in (0, 4)]

    places = jnp.arange(8)
    offset = jnp.where(core == 0, places - y, y - places) % 8
    at_offset = jnp.array([0, 4, 2, 6, 1, 5, 3, 7])[offset]
    column = jnp.take(column, at_offset, axis=0).reshape(144, D)
    own_t = spread(column, "seq", GROUPS_CHIP).reshape(8, 144, D)
    other_t = lax.ppermute(own_t, "seq", SWAP)

    full_order = model_order()
    small_order = context_order()
    expand = expand_order()
    cot_p = to_patches(out_grad)

    hidden, qkv, probs_s, context_s = call(
        forward_kernel,
        [tokens_b, ((3, TOKENS, PAD), BF), (probs, F32), ((TOKENS, PAD), BF)],
        [pltpu.VMEM((2 * D, D), BF), sems],
        700_000_000,
        at, x, expand, *blocks, *swapped,
        hbm=range(3, 13),
    )
    hidden_p = to_patches(hidden)
    mixed_p, grad_p, share = call(
        temporal_kernel,
        [tokens_b, tokens_b, ((WIDTH, D), BF)],
        [pltpu.VMEM((ALL_ROWS, D), BF), pltpu.VMEM(probs, F32), sems],
        1_600_000_000,
        at, hidden_p, cot_p, own_t, other_t, small_order, full_order,
        hbm=(3, 4),
    )
    grad = to_patches(grad_p)
    (input_grad,) = call(
        backward_kernel,
        [tokens_b],
        [pltpu.VMEM((2 * D, D), BF), sems],
        800_000_000,
        at, x, grad, qkv, probs_s, context_s, expand, *blocks, *swapped,
        hbm=range(7, 17),
    )
    mixed = to_patches(mixed_p)

    share = share.reshape(2, SHARE, D)
    keep = lax.dynamic_index_in_dim(share, core, 0, keepdims=False)
    send = lax.dynamic_index_in_dim(share, 1 - core, 0, keepdims=False)
    both = (keep.astype(F32) + lax.ppermute(send, "seq", SWAP).astype(F32)).astype(BF)
    both = both.reshape(2, 8, 2, 9, D).transpose(1, 0, 2, 3, 4).reshape(8, 36, D)
    over_y = lax.all_to_all(both, "dp", 0, 0, axis_index_groups=GROUPS_Y, tiled=True)
    over_y = jnp.sum(over_y.astype(F32), axis=0).astype(BF).reshape(4, 9, D)
    over_z = lax.all_to_all(over_y, "dp", 0, 0, axis_index_groups=GROUPS_Z, tiled=True)
    over_z = jnp.sum(over_z.astype(F32), axis=0).astype(BF)
    over_seq = spread(over_z, "seq", [list(range(16))]).reshape(8, 2, 9, D)
    out_temporal_grad = jnp.sum(over_seq.astype(F32), axis=0).reshape(18, D)

    return mixed[None, None], input_grad[None, None], out_temporal_grad


def solution(mesh):
    tokens = P("dp", "seq", None, None)
    placed = (tokens, P(None, "dp", None), P("dp", None), P(None, "dp", None), P("dp", None), tokens)
    return jax.shard_map(
        per_device,
        mesh=mesh,
        in_specs=placed,
        out_specs=(tokens, tokens, P("dp", None)),
        check_vma=False,
    )
```

```python
import jax
import jax.numpy as jnp
from jax import lax
from jax.experimental import pallas as pl
from jax.experimental.pallas import tpu as pltpu
from jax.sharding import PartitionSpec as P

BF = jnp.bfloat16
F32 = jnp.float32
EPSILON = 1e-06
D = 1152
WIDTH = 576
PAD = 640
HEADS = 8
HEAD = 72
TOKENS = 128
PATCH_BLOCK = 8
SCALING = HEAD ** (-0.5)
SHARE = 288
V_ROWS, ALL_ROWS = 1152, 2304
VMEM_LIMIT = 60 * 1024 * 1024


def nn(a, b):
    return lax.dot_general(a, b, (((1,), (0,)), ((), ())), preferred_element_type=F32)


def nt(a, b):
    return lax.dot_general(a, b, (((1,), (1,)), ((), ())), preferred_element_type=F32)


def tn(a, b):
    return lax.dot_general(a, b, (((0,), (0,)), ((), ())), preferred_element_type=F32)


def lanes(shape):
    return lax.broadcasted_iota(jnp.int32, shape, len(shape) - 1)


def normalize(values):
    centred = values - jnp.mean(values, axis=-1, keepdims=True)
    inverse = lax.rsqrt(jnp.mean(centred * centred, axis=-1, keepdims=True) + EPSILON)
    return centred * inverse, inverse


def norm_back(grad, normed, inverse):
    return inverse * (
        grad
        - jnp.mean(grad, axis=-1, keepdims=True)
        - normed * jnp.mean(grad * normed, axis=-1, keepdims=True)
    )


def keep_width(a):
    return jnp.where(lanes(a.shape) < WIDTH, a, 0.0)


def window(h):
    low = h * HEAD // 128 * 128
    high = -(-(h * HEAD + HEAD) // 128) * 128
    return low, high


def head_mask(h):
    low, high = window(h)
    at = lanes((TOKENS, high - low)) + low
    return (at >= h * HEAD) & (at < h * HEAD + HEAD)


def add_window(tiles, h, part):
    low, high = window(h)
    part = jnp.where(head_mask(h), part, 0.0)
    for t in range(low // 128, high // 128):
        piece = part[:, t * 128 - low : t * 128 - low + 128]
        tiles[t] = piece if tiles[t] is None else tiles[t] + piece


def join(tiles):
    return jnp.concatenate(tiles, axis=1)


def halves(a):
    return keep_width(a[:, :PAD]), keep_width(pltpu.roll(a, WIDTH, 1)[:, :PAD])


def whole(first, second):
    zeros = jnp.zeros((TOKENS, D - PAD), F32)
    first = jnp.concatenate([keep_width(first), zeros], axis=1)
    second = jnp.concatenate([keep_width(second), zeros], axis=1)
    return first + pltpu.roll(second, WIDTH, 1)


def project_temporal(normed, weights):
    normed_b = normed.astype(BF)
    q = nn(normed_b, weights[0, :V_ROWS])
    k = nn(normed_b, weights[1, :V_ROWS])
    first, second = halves(normed)
    v = nn(first.astype(BF), weights[0, V_ROWS : V_ROWS + PAD])
    v = v + nn(second.astype(BF), weights[1, V_ROWS : V_ROWS + PAD])
    return q.astype(BF), k.astype(BF), v.astype(BF)


def back_project_temporal(dq, dk, dv, weights):
    grad = nt(dq.astype(BF), weights[0, :V_ROWS]) + nt(dk.astype(BF), weights[1, :V_ROWS])
    dv = dv.astype(BF)
    first = nt(dv, weights[0, V_ROWS : V_ROWS + PAD])
    second = nt(dv, weights[1, V_ROWS : V_ROWS + PAD])
    return grad + whole(first, second)


def rounded(a):
    return a.astype(BF).astype(F32)


def attend(q, k, v, allowed, probs_ref):
    tiles = [None] * (PAD // 128)
    for h in range(HEADS):
        low, high = window(h)
        masked = jnp.where(head_mask(h), q[:, low:high].astype(F32), 0.0).astype(BF)
        scores = nt(masked, k[:, low:high]) * SCALING
        if allowed is not None:
            scores = jnp.where(allowed, scores, -1e38)
        powers = jnp.exp(scores - jnp.max(scores, axis=-1, keepdims=True))
        probs = powers / jnp.sum(powers, axis=-1, keepdims=True)
        probs_ref[h] = probs
        add_window(tiles, h, nn(probs.astype(BF), v[:, low:high]))
    return join(tiles).astype(BF)


def attend_back(q, k, v, context, context_grad, probs_ref):
    dq, dk, dv = ([None] * (PAD // 128) for _ in range(3))
    for h in range(HEADS):
        low, high = window(h)
        grad = context_grad[:, low:high]
        masked = jnp.where(head_mask(h), grad.astype(F32), 0.0)
        probs = probs_ref[h]
        prob_grad = nt(masked.astype(BF), v[:, low:high])
        row = jnp.sum(masked * context[:, low:high].astype(F32), axis=-1, keepdims=True)
        score_grad = (probs * (prob_grad - row) * SCALING).astype(BF)
        add_window(dv, h, tn(probs.astype(BF), grad))
        add_window(dq, h, nn(score_grad, k[:, low:high]))
        add_window(dk, h, tn(score_grad, q[:, low:high]))
    return rounded(join(dq)), rounded(join(dk)), rounded(join(dv))


def start_all(copies):
    for copy in copies:
        copy.start()
    return copies


def wait_all(copies):
    for copy in copies:
        copy.wait()


def load_spatial(at_ref, blocks, weights, sems):
    y, core = at_ref[0], at_ref[1]
    sign = 1 - 2 * core
    groups = []
    for half in range(2):
        rows = pl.ds(half * 144, 144)
        parts = [(blocks[0].at[rows, :], half, y)]
        for step in range(1, 4):
            parts.append((blocks[step].at[rows, :], half, y - sign * step))
            parts.append((blocks[3 + step].at[rows, :], half, y + sign * step))
        parts.append((blocks[7 + half], core if half == 0 else 1 - core, y + 4))
        copies = []
        for n, (source, part, place) in enumerate(parts):
            at = pl.multiple_of(part * D + lax.rem(place + 16, 8) * 144, 144)
            copies.append(
                pltpu.make_async_copy(
                    source, weights.at[pl.ds(at, 144), :], sems.at[half * 8 + n]
                )
            )
        groups.append(start_all(copies))
    return groups


def load_temporal(at_ref, blocks, weights, sems):
    core, x, z = at_ref[1], at_ref[2] % 4, at_ref[2] // 4
    copies = []
    for n, block in enumerate(blocks):
        half = core if n < 4 else 1 - core
        place = lax.rem(x + (0, -1, 1, 2)[n % 4] * (1 - 2 * half) + 4, 4)
        for entry in range(2):
            share = (z if entry == 0 else 1 - z) * 4 + place
            at = pl.multiple_of(share * SHARE, SHARE)
            copies.append(
                pltpu.make_async_copy(
                    block.at[pl.ds(entry * SHARE, SHARE), :],
                    weights.at[half, pl.ds(at, SHARE), :],
                    sems.at[len(copies)],
                )
            )
    return start_all(copies)


def project_spatial(normed, weights, groups):
    normed_b = normed.astype(BF)
    wait_all(groups[0] + groups[1][-1:])
    qk = nn(normed_b, weights[:D, :])
    wait_all(groups[1][:-1])
    v = keep_width(nn(normed_b, weights[D:, :PAD]))
    k = pltpu.roll(qk, WIDTH, 1)
    return qk[:, :PAD].astype(BF), k[:, :PAD].astype(BF), v.astype(BF)


def pair_lanes(dq, dk):
    zeros = jnp.zeros((TOKENS, D - PAD), F32)
    return jnp.concatenate([dq, zeros], axis=1) + pltpu.roll(
        jnp.concatenate([dk, zeros], axis=1), WIDTH, 1
    )


def back_project_spatial(dq, dk, dv, weights):
    return nt(pair_lanes(dq, dk).astype(BF), weights[:D, :]) + nt(
        dv.astype(BF), weights[D:, :PAD]
    )


def late(a):
    return jnp.where(lanes(a.shape) >= PAD - WIDTH, a, 0.0)


def out_spatial_of(context, expand, weights):
    zeros = jnp.zeros((TOKENS, D - PAD), F32)
    spread_out = nn(context, expand)
    first = late(nn(spread_out.astype(BF), weights[D:, D - PAD :]))
    second = late(nn(pltpu.roll(spread_out, 18, 1).astype(BF), weights[D:, D - PAD :]))
    return pltpu.roll(
        jnp.concatenate([first, zeros], axis=1), D - (PAD - WIDTH), 1
    ) + jnp.concatenate([zeros, second], axis=1)


def context_grad_spatial(grad, expand, weights):
    first = late(pltpu.roll(grad, PAD - WIDTH, 1)[:, :PAD])
    second = late(grad[:, D - PAD :])
    total = nt(first.astype(BF), weights[D:, D - PAD :]) + pltpu.roll(
        nt(second.astype(BF), weights[D:, D - PAD :]), D - 18, 1
    )
    return nt(total.astype(BF), expand).astype(BF)


def selection(rows, columns, shift):
    r = lax.broadcasted_iota(jnp.int32, (rows, columns), 0)
    c = lax.broadcasted_iota(jnp.int32, (rows, columns), 1)
    return r + shift == c


def pack_kernel(at_ref, *refs):
    outside, inside_refs, sems = refs[:4], refs[6:10], refs[10]
    all_ref, half_ref = refs[4:6]
    wait_all(
        start_all(
            [
                pltpu.make_async_copy(a, b, sems.at[n])
                for n, (a, b) in enumerate(zip(outside, inside_refs))
            ]
        )
    )
    qkv_s, out_s, qkv_t, out_t = inside_refs
    chip, core = at_ref[2], at_ref[1]

    def pick(which, a):
        return nn(which.astype(F32).astype(BF), a)

    def side(a, b):
        return jnp.concatenate([a, b], axis=1)

    def rows(count, at, size):
        return selection(count, size, at)

    q, k, v, out = qkv_s[0], qkv_s[1], qkv_s[2], out_s[...]
    lead = selection(36, 18, 0)
    tail = selection(36, 18, -18)
    halves = pick(lead, out[:, :WIDTH]) + pick(tail, out[:, WIDTH:])
    first = side(q.astype(F32), k.astype(F32))
    second = side(v.astype(F32), halves)
    q, k, v, out = qkv_t[0], qkv_t[1], qkv_t[2], out_t[...]
    nine = lax.broadcasted_iota(jnp.int32, (16, 1), 0) < 9

    def inside(low, high):
        return nine & (chip >= low) & (chip < high)

    here = rows(16, chip * 9, 36) & inside(0, 4)
    upper = rows(16, (chip - 4) * 9, 36) & inside(4, 6)
    lower = rows(16, (chip - 4) * 9 + 18, 36) & inside(4, 6)
    last = rows(16, (chip - 6) * 9, 18) & inside(6, 8)
    temporal = side(pick(here, q) + pick(upper, v), pick(here, k) + pick(lower, v))
    temporal = temporal + pick(last, out)
    half = jnp.where(core == 0, first, second)
    half_ref[...] = jnp.concatenate([half, temporal], axis=0).astype(BF)
    all_ref[...] = jnp.concatenate([first, second, temporal], axis=0).astype(BF)


def column_kernel(at_ref, own_ref, next_ref, far_ref, other_ref, block_ref, share_ref):
    z, core = at_ref[3], at_ref[1]
    own, near, far = (ref[...].astype(F32) for ref in (own_ref, next_ref, far_ref))
    other = other_ref[...].astype(F32)
    below = jnp.where(core == 0, near, other[:88])
    above = jnp.where(core == 0, other[:88], near)
    far_low = jnp.where(core == 0, far[:36], other[88:124])
    far_high = jnp.where(core == 0, other[88:124], far[:36])
    low, high, share = [], [], []
    for place in range(4):
        distance = lax.rem(place - z + 4, 4)

        def choose(a, b):
            part = jnp.where(distance == 0, own[a], jnp.where(distance == 1, above[a], b))
            return jnp.where(distance == 3, below[a], part)

        low.append(choose(slice(0, 36), far_low))
        high.append(choose(slice(36, 72), far_high))
        share.append(choose(slice(72, 81), far[36:45]))
    block_ref[...] = jnp.concatenate(low + high, axis=0).astype(BF)
    share = jnp.concatenate(share, axis=0)
    share = jnp.where(core == 0, share, pltpu.roll(share, WIDTH, 1))[:, :PAD]
    share = keep_width(share).astype(BF)
    for y in range(8):
        share_ref[y] = share


def forward_kernel(*refs):
    (at_ref, x_ref, cot_ref, expand_ref), refs = refs[:4], refs[4:]
    blocks, refs = refs[:9], refs[9:]
    both_ref, *outside, weights, qkv_ref, probs_ref, context_ref, sems = refs
    groups = load_spatial(at_ref, blocks, weights, sems)
    both_ref[:, D:] = cot_ref[...]
    x = x_ref[...].astype(F32)
    q, k, v = project_spatial(normalize(x)[0], weights, groups)
    qkv_ref[0], qkv_ref[1], qkv_ref[2] = q, k, v
    context = attend(q, k, v, None, probs_ref)
    context_ref[...] = context
    copies = start_all(
        [
            pltpu.make_async_copy(a, b, sems.at[n])
            for n, (a, b) in enumerate(zip((qkv_ref, probs_ref, context_ref), outside))
        ]
    )
    both_ref[:, :D] = (x + out_spatial_of(context, expand_ref[...], weights)).astype(BF)
    wait_all(copies)


def temporal_kernel(at_ref, both_ref, full_ref, share_order_ref, *refs):
    keep_ref, send_ref, qkv_ref, probs_ref, context_ref, weights, sems = refs[8:]
    copies = load_temporal(at_ref, refs[:8], weights, sems)
    normed = normalize(both_ref[:, :D].astype(F32))[0]
    ordered = nn(normed.astype(BF), full_ref[...])
    wait_all(copies)
    q, k, v = project_temporal(ordered, weights)
    qkv_ref[0], qkv_ref[1], qkv_ref[2] = q, k, v
    rows = lax.broadcasted_iota(jnp.int32, (TOKENS, TOKENS), 0)
    cols = lax.broadcasted_iota(jnp.int32, (TOKENS, TOKENS), 1)
    allowed = (rows & (PATCH_BLOCK - 1)) == (cols & (PATCH_BLOCK - 1))
    context = attend(q, k, v, allowed, probs_ref)
    context_ref[...] = context
    share = tn(nn(context, share_order_ref[...]).astype(BF), both_ref[:, D:]).astype(BF)
    keep_ref[...], send_ref[...] = share[:SHARE], share[SHARE:WIDTH]


def temporal_back_kernel(
    at_ref, both_ref, qkv_ref, probs_ref, context_ref, order_ref, full_ref, *refs
):
    back_ref, weights, sems = refs[8:]
    copies = load_temporal(at_ref, refs[:8], weights, sems)
    hidden, cot = both_ref[:, :D].astype(F32), both_ref[:, D:].astype(F32)
    normed, inverse = normalize(hidden)
    context, order, full = context_ref[...], order_ref[...], full_ref[...]
    ordered = nn(context, order).astype(BF)
    wait_all(copies)
    left, right = weights[0, ALL_ROWS - PAD :], weights[1, ALL_ROWS - PAD :]
    back_ref[:, D:] = (hidden + whole(nn(ordered, left), nn(ordered, right))).astype(BF)
    first, second = halves(cot)
    context_grad = nt(first.astype(BF), left) + nt(second.astype(BF), right)
    context_grad = nt(context_grad.astype(BF), order).astype(BF)
    dq, dk, dv = attend_back(
        qkv_ref[0], qkv_ref[1], qkv_ref[2], context, context_grad, probs_ref
    )
    normed_grad = nt(back_project_temporal(dq, dk, dv, weights).astype(BF), full)
    back_ref[:, :D] = (cot + norm_back(normed_grad, normed, inverse)).astype(BF)


def backward_kernel(*refs):
    (at_ref, x_ref, both_ref, qkv_ref, probs_ref, context_ref, expand_ref), refs = refs[:7], refs[7:]
    blocks, refs = refs[:9], refs[9:]
    input_grad_ref, weights, sems = refs
    first, second = load_spatial(at_ref, blocks, weights, sems)
    normed, inverse = normalize(x_ref[...].astype(F32))
    wait_all(first + second)
    grad = both_ref[:, :D].astype(F32)
    context_grad = context_grad_spatial(grad, expand_ref[...], weights)
    dq, dk, dv = attend_back(
        qkv_ref[0], qkv_ref[1], qkv_ref[2], context_ref[...], context_grad, probs_ref
    )
    normed_grad = back_project_spatial(dq, dk, dv, weights)
    input_grad_ref[...] = (grad + norm_back(normed_grad, normed, inverse)).astype(BF)


def call(kernel, outs, scratch, micros, *args, smem=True, hbm=(), hbm_outs=()):
    in_specs = []
    for at in range(len(args)):
        space = pltpu.VMEM
        if smem and at == 0:
            space = pltpu.SMEM
        elif at in hbm:
            space = pl.ANY
        in_specs.append(pl.BlockSpec(memory_space=space))
    return pl.pallas_call(
        kernel,
        out_shape=[jax.ShapeDtypeStruct(s, t) for s, t in outs],
        in_specs=in_specs,
        out_specs=[
            pl.BlockSpec(memory_space=pl.ANY if n in hbm_outs else pltpu.VMEM)
            for n in range(len(outs))
        ],
        scratch_shapes=scratch,
        compiler_params=pltpu.CompilerParams(vmem_limit_bytes=VMEM_LIMIT),
        cost_estimate=pl.CostEstimate(
            flops=micros * 1_100_000_000, bytes_accessed=3_000_000, transcendentals=0
        ),
    )(*args)


def model_order():
    n = jnp.arange(D)
    dp, row = n // 36, n % 36
    at = (row // 9) * SHARE + dp * 9 + row % 9
    return (at[:, None] == jnp.arange(D)[None, :]).astype(BF)


def context_order():
    f = jnp.arange(PAD)
    dp, row = f // 18, f % 18
    at = PAD - WIDTH + (row // 9) * SHARE + dp * 9 + row % 9
    at = jnp.where(f < WIDTH, at, -1)
    return (at[:, None] == jnp.arange(PAD)[None, :]).astype(BF)


def share_order(y, core):
    f = jnp.arange(PAD)
    dp, row = f // 18, f % 18
    half = row // 9
    away = jnp.where(half == 0, dp // 4 - y, y - dp // 4) % 4
    far = away % 2 * 144 + away // 2 * 72 + jnp.where(half == core, 0, SHARE)
    at = far + dp // 16 * 36 + dp % 4 * 9 + row % 9
    at = jnp.where(f < WIDTH, at, -1)
    return (at[:, None] == jnp.arange(PAD)[None, :]).astype(BF)


def expand_order():
    f = jnp.arange(PAD)
    at = jnp.where(f < WIDTH, 36 * (f // 18) + f % 18, -1)
    return (at[:, None] == jnp.arange(D)[None, :]).astype(BF)


GROUPS_Z = [[y * 4 + z for z in range(4)] for y in range(8)]
GROUPS_Y = [[y * 4 + z for y in range(8)] for z in range(4)]
GROUPS_FAR = [[y * 4 + z for y in (p, p + 4) for z in range(4)] for p in range(4)]
SWAP = [(s, s ^ 1) for s in range(16)]
ACROSS = [(s, s ^ 8) for s in range(16)]


def spread(block, axis, groups):
    count = len(groups[0])
    return lax.all_to_all(
        jnp.broadcast_to(block[None], (count,) + block.shape), axis, 0, 0,
        axis_index_groups=groups, tiled=True,
    )


def along_z(distance):
    pairs = []
    for y in range(8):
        for z in range(4):
            for s in range(16):
                to = (z + (distance if s % 2 == 0 else -distance)) % 4
                pairs.append(((y * 4 + z) * 16 + s, (y * 4 + to) * 16 + s))
    return pairs


def along_y(distance):
    pairs = []
    for y in range(8):
        for z in range(4):
            for s in range(16):
                to = (y + (distance if s % 2 == 0 else -distance)) % 8
                pairs.append(((y * 4 + z) * 16 + s, (to * 4 + z) * 16 + s))
    return pairs


def along_x(distance):
    pairs = []
    for s in range(16):
        to = (s // 2 + (distance if s % 2 == 0 else -distance)) % 4
        pairs.append((s, s // 8 * 8 + to * 2 + s % 2))
    return pairs


UP = along_y(1)


def move(a, pairs):
    return lax.ppermute(a, ("dp", "seq"), pairs)


def per_device(clips, qkv_spatial, out_spatial, qkv_temporal, out_temporal, cotangent):
    x = clips.reshape(TOKENS, D)
    out_grad = cotangent.reshape(TOKENS, D)
    seq, dp = lax.axis_index("seq"), lax.axis_index("dp")
    y, chip, core = dp // 4, seq // 2, seq % 2
    at = jnp.stack([y, core, chip, dp % 4]).astype(jnp.int32)

    tokens_b = ((TOKENS, D), BF)
    wide_b = ((TOKENS, 2 * D), BF)
    probs = (HEADS, TOKENS, TOKENS)
    sems = pltpu.SemaphoreType.DMA((16,))

    def turn(a):
        parts = a.reshape(16, PATCH_BLOCK, 2 * D)
        return lax.all_to_all(parts, "seq", 0, 0, tiled=True).reshape(TOKENS, 2 * D)

    packed, packed_h = call(
        pack_kernel, [((88, D), BF), ((52, D), BF)],
        [
            pltpu.VMEM((3, 36, WIDTH), BF), pltpu.VMEM((18, D), BF),
            pltpu.VMEM((3, 36, WIDTH), BF), pltpu.VMEM((18, D), BF), sems,
        ],
        2, at, qkv_spatial, out_spatial, qkv_temporal, out_temporal, hbm=range(1, 5),
    )
    orders = model_order(), context_order(), share_order(y, core), expand_order()
    near, far = move(packed, along_z(1)), move(packed_h, along_z(2))

    def swap(a):
        return lax.ppermute(a, "seq", SWAP)

    block, shares = call(
        column_kernel, [((2 * 144, D), BF), ((8, 36, PAD), BF)], [], 2,
        at, packed, near, far, swap(jnp.concatenate([near, far])),
    )
    shares = lax.all_to_all(shares, "dp", 0, 0, axis_index_groups=GROUPS_Y, tiled=True)
    shares = shares.reshape(SHARE, PAD)

    ring, theirs = [block], []
    for step in range(1, 4):
        ring.append(move(ring[-1], UP))
        if step == 1:
            ring[1], *orders = lax.optimization_barrier((ring[1], *orders))
        else:
            theirs.append(swap(ring[step - 1]))
            ring[step], theirs[-1] = lax.optimization_barrier((ring[step], theirs[-1]))
    full_order, small_order, wgrad_order, expand = orders
    last = move(lax.dynamic_slice_in_dim(ring[3], core * 144, 144, axis=0), UP)
    theirs.append(swap(ring[3]))
    last, theirs[2] = lax.optimization_barrier((last, theirs[2]))

    def round_x(a, distance):
        return lax.ppermute(a, "seq", along_x(distance))

    pair = jnp.concatenate([shares, lax.ppermute(shares, "seq", ACROSS)])
    after = round_x(pair, 1)
    blocks_t = [pair, after, round_x(pair, -1), round_x(after, 1)]
    blocks_t += list(map(swap, blocks_t))
    blocks = [*ring, *theirs, last, swap(last)]

    both, qkv, probs_s, context_s = call(
        forward_kernel,
        [wide_b, ((3, TOKENS, PAD), BF), (probs, F32), ((TOKENS, PAD), BF)],
        [
            pltpu.VMEM((2 * D, D), BF), pltpu.VMEM((3, TOKENS, PAD), BF), pltpu.VMEM(probs, F32),
            pltpu.VMEM((TOKENS, PAD), BF), sems,
        ],
        8,
        at, x, out_grad, expand, *blocks,
        hbm=range(4, 13), hbm_outs=(1, 2, 3),
    )
    both = turn(both)
    saved = [((3, TOKENS, PAD), BF), (probs, F32), ((TOKENS, PAD), BF)]
    temporal_weights = pltpu.VMEM((2, ALL_ROWS, PAD), BF)
    keep, send, *saved_t = call(
        temporal_kernel, [((SHARE, D), BF), ((SHARE, D), BF), *saved], [temporal_weights, sems], 8,
        at, both, full_order, wgrad_order, *blocks_t, hbm=range(4, 12),
    )

    def add(a, b):
        return (a.astype(F32) + b.astype(F32)).astype(BF)

    total = add(keep, swap(send))
    both, total = lax.optimization_barrier((both, total))
    (both_back,) = call(
        temporal_back_kernel, [wide_b], [temporal_weights, sems], 9,
        at, both, *saved_t, small_order, full_order, *blocks_t, hbm=range(7, 15),
    )
    both_back = turn(both_back)
    total = add(total[:144], move(total[144:], UP))
    total = add(total[:72], move(total[72:], along_y(2)))
    total, both_back = lax.optimization_barrier((total, both_back))
    (input_grad,) = call(
        backward_kernel,
        [tokens_b],
        [pltpu.VMEM((2 * D, D), BF), sems],
        9,
        at, x, both_back, qkv, probs_s, context_s, expand, *blocks,
        hbm=range(7, 16),
    )
    over_z = lax.all_to_all(
        total.reshape(8, 9, D), "dp", 0, 0, axis_index_groups=GROUPS_FAR, tiled=True
    )
    over_z = jnp.sum(over_z.astype(F32), axis=0).astype(BF)
    over_z, input_grad = lax.optimization_barrier((over_z, input_grad))
    over_seq = spread(over_z, "seq", [list(range(16))]).reshape(8, 2, 9, D)
    out_temporal_grad = jnp.sum(over_seq.astype(F32), axis=0).reshape(18, D)
    mixed = both_back[:, D:]

    return mixed[None, None], input_grad[None, None], out_temporal_grad


def solution(mesh):
    tokens = P("dp", "seq", None, None)
    placed = (tokens, P(None, "dp", None), P("dp", None), P(None, "dp", None), P("dp", None), tokens)
    return jax.shard_map(
        per_device,
        mesh=mesh,
        in_specs=placed,
        out_specs=(tokens, tokens, P("dp", None)),
        check_vma=False,
    )
```

```python
import jax
import jax.numpy as jnp
from jax import lax
from jax.experimental import pallas as pl
from jax.experimental.pallas import tpu as pltpu
from jax.sharding import PartitionSpec as P

BF = jnp.bfloat16
F32 = jnp.float32
EPSILON = 1e-06
D = 1152
WIDTH = 576
PAD = 640
HEADS = 8
HEAD = 72
TOKENS = 128
PATCH_BLOCK = 8
SCALING = HEAD ** (-0.5)
SHARE = 288
BLOCK = 144
VMEM_LIMIT = 62 * 1024 * 1024


def nn(a, b):
    return lax.dot_general(a, b, (((1,), (0,)), ((), ())), preferred_element_type=F32)


def nt(a, b):
    return lax.dot_general(a, b, (((1,), (1,)), ((), ())), preferred_element_type=F32)


def tn(a, b):
    return lax.dot_general(a, b, (((0,), (0,)), ((), ())), preferred_element_type=F32)


def lanes(shape):
    return lax.broadcasted_iota(jnp.int32, shape, len(shape) - 1)


def normalize(values):
    centred = values - jnp.mean(values, axis=-1, keepdims=True)
    inverse = lax.rsqrt(jnp.mean(centred * centred, axis=-1, keepdims=True) + EPSILON)
    return centred * inverse, inverse


def norm_back(grad, normed, inverse):
    return inverse * (
        grad
        - jnp.mean(grad, axis=-1, keepdims=True)
        - normed * jnp.mean(grad * normed, axis=-1, keepdims=True)
    )


def keep_width(a):
    return jnp.where(lanes(a.shape) < WIDTH, a, 0.0)


def window(h):
    low = h * HEAD // 128 * 128
    high = -(-(h * HEAD + HEAD) // 128) * 128
    return low, high


def head_mask(h):
    low, high = window(h)
    at = lanes((TOKENS, high - low)) + low
    return (at >= h * HEAD) & (at < h * HEAD + HEAD)


def add_window(tiles, h, part):
    low, high = window(h)
    part = jnp.where(head_mask(h), part, 0.0)
    for t in range(low // 128, high // 128):
        piece = part[:, t * 128 - low : t * 128 - low + 128]
        tiles[t] = piece if tiles[t] is None else tiles[t] + piece


def join(tiles):
    return jnp.concatenate(tiles, axis=1)


def rounded(a):
    return a.astype(BF).astype(F32)


def attend(q, k, v, allowed, probs_ref):
    tiles = [None] * (PAD // 128)
    for h in range(HEADS):
        low, high = window(h)
        masked = jnp.where(head_mask(h), q[:, low:high].astype(F32), 0.0).astype(BF)
        scores = nt(masked, k[:, low:high]) * SCALING
        if allowed is not None:
            scores = jnp.where(allowed, scores, -1e38)
        powers = jnp.exp(scores - jnp.max(scores, axis=-1, keepdims=True))
        probs = powers / jnp.sum(powers, axis=-1, keepdims=True)
        probs_ref[h] = probs
        add_window(tiles, h, nn(probs.astype(BF), v[:, low:high]))
    return join(tiles).astype(BF)


def attend_back(q, k, v, context, context_grad, probs_ref):
    dq, dk, dv = ([None] * (PAD // 128) for _ in range(3))
    for h in range(HEADS):
        low, high = window(h)
        grad = context_grad[:, low:high]
        masked = jnp.where(head_mask(h), grad.astype(F32), 0.0)
        probs = probs_ref[h]
        prob_grad = nt(masked.astype(BF), v[:, low:high])
        row = jnp.sum(masked * context[:, low:high].astype(F32), axis=-1, keepdims=True)
        score_grad = (probs * (prob_grad - row) * SCALING).astype(BF)
        add_window(dv, h, tn(probs.astype(BF), grad))
        add_window(dq, h, nn(score_grad, k[:, low:high]))
        add_window(dk, h, tn(score_grad, q[:, low:high]))
    return rounded(join(dq)), rounded(join(dk)), rounded(join(dv))


def start_all(copies):
    for copy in copies:
        copy.start()
    return copies


def wait_all(copies):
    for copy in copies:
        copy.wait()


def load_weights(at_ref, blocks, weights, sems, order):
    y, core = at_ref[0], at_ref[1]
    sign = 1 - 2 * core

    def copy(source, half, place, sem):
        at = pl.multiple_of(half * D + lax.rem(place + 16, 8) * BLOCK, BLOCK)
        return pltpu.make_async_copy(source, weights.at[pl.ds(at, BLOCK), :], sems.at[sem])

    last = start_all([copy(blocks[7], core, y + 4, 0), copy(blocks[8], 1 - core, y + 4, 8)])
    groups = {}
    for half in order:
        rows = pl.ds(half * BLOCK, BLOCK)
        copies = [copy(blocks[0].at[rows, :], half, y, half * 8 + 1)]
        for step in range(1, 4):
            below, above = blocks[step].at[rows, :], blocks[3 + step].at[rows, :]
            copies.append(copy(below, half, y - sign * step, half * 8 + 2 * step))
            copies.append(copy(above, half, y + sign * step, half * 8 + 2 * step + 1))
        groups[half] = start_all(copies)
    groups[order[0]] = last + groups[order[0]]
    return groups


def project(normed, weights, wait_first, wait_second):
    normed_b = normed.astype(BF)
    wait_first()
    qk = nn(normed_b, weights[:D, :])
    wait_second()
    v = keep_width(nn(normed_b, weights[D:, :PAD]))
    k = pltpu.roll(qk, WIDTH, 1)
    return qk[:, :PAD].astype(BF), k[:, :PAD].astype(BF), v.astype(BF)


def pair_lanes(dq, dk):
    zeros = jnp.zeros((TOKENS, D - PAD), F32)
    return jnp.concatenate([dq, zeros], axis=1) + pltpu.roll(
        jnp.concatenate([dk, zeros], axis=1), WIDTH, 1
    )


def back_project(dq, dk, dv, weights):
    return nt(pair_lanes(dq, dk).astype(BF), weights[:D, :]) + nt(dv.astype(BF), weights[D:, :PAD])


def late(a):
    return jnp.where(lanes(a.shape) >= PAD - WIDTH, a, 0.0)


def out_weights(weights, side):
    starts = [D + y * BLOCK + side * 72 for y in range(8)]
    return jnp.concatenate([weights[at : at + 72, D - PAD :] for at in starts], axis=0)


def project_out(context, left, right):
    zeros = jnp.zeros((TOKENS, D - PAD), F32)
    context = context[:, :WIDTH]
    first, second = late(nn(context, left)), late(nn(context, right))
    return pltpu.roll(
        jnp.concatenate([first, zeros], axis=1), D - (PAD - WIDTH), 1
    ) + jnp.concatenate([zeros, second], axis=1)


def back_project_out(grad, left, right):
    first = late(pltpu.roll(grad, PAD - WIDTH, 1)[:, :PAD])
    second = late(grad[:, D - PAD :])
    context_grad = nt(first.astype(BF), left) + nt(second.astype(BF), right)
    return jnp.concatenate([context_grad, jnp.zeros((TOKENS, PAD - WIDTH), F32)], axis=1).astype(BF)


def selection(rows, columns, shift):
    r = lax.broadcasted_iota(jnp.int32, (rows, columns), 0)
    c = lax.broadcasted_iota(jnp.int32, (rows, columns), 1)
    return r + shift == c


def pack_kernel(at_ref, *refs):
    outside, inside_refs, sems = refs[:4], refs[8:12], refs[12]
    wait_all(
        start_all(
            [
                pltpu.make_async_copy(a, b, sems.at[n])
                for n, (a, b) in enumerate(zip(outside, inside_refs))
            ]
        )
    )
    qkv_s, out_s, qkv_t, out_t = inside_refs
    core = at_ref[1]

    def pick(which, a):
        return nn(which.astype(F32).astype(BF), a)

    def side(a, b):
        return jnp.concatenate([a, b], axis=1)

    lead = selection(36, 18, 0)
    tail = selection(36, 18, -18)

    def blocks(qkv, out_ref):
        q, k, v, out = qkv[0], qkv[1], qkv[2], out_ref[...]
        halves = pick(lead, out[:, :WIDTH]) + pick(tail, out[:, WIDTH:])
        return side(q.astype(F32), k.astype(F32)), side(v.astype(F32), halves)

    for n, (qkv, out_ref) in enumerate(((qkv_s, out_s), (qkv_t, out_t))):
        all_ref, half_ref = refs[4 + 2 * n : 6 + 2 * n]
        first, second = blocks(qkv, out_ref)
        half_ref[...] = jnp.where(core == 0, first, second).astype(BF)
        all_ref[...] = jnp.concatenate([first, second], axis=0).astype(BF)


def in_sides(parts):
    plain = jnp.concatenate(parts, axis=0)
    by_side = jnp.concatenate([p[:18] for p in parts] + [p[18:] for p in parts], axis=0)
    return jnp.where(lanes(plain.shape) < WIDTH, plain, by_side)


def in_order(z, own, below, above, far):
    parts = []
    for place in range(4):
        distance = lax.rem(place - z + 4, 4)
        part = jnp.where(distance == 0, own, jnp.where(distance == 1, above, far))
        parts.append(jnp.where(distance == 3, below, part))
    return parts


def column_kernel(at_ref, own_ref, next_ref, far_ref, other_ref, block_ref):
    z, core = at_ref[3], at_ref[1]
    own, near, far = (ref[...].astype(F32) for ref in (own_ref, next_ref, far_ref))
    other = other_ref[...].astype(F32)
    below = jnp.where(core == 0, near, other[:72])
    above = jnp.where(core == 0, other[:72], near)
    low = jnp.where(core == 0, far, other[72:])
    high = jnp.where(core == 0, other[72:], far)
    first = in_order(z, own[:36], below[:36], above[:36], low)
    second = in_order(z, own[36:], below[36:], above[36:], high)
    block_ref[:BLOCK] = jnp.concatenate(first, axis=0).astype(BF)
    block_ref[BLOCK:] = in_sides(second).astype(BF)


def fetch(pairs, sems):
    return start_all(
        [pltpu.make_async_copy(a, b, sems.at[n]) for n, (a, b) in enumerate(pairs)]
    )


def forward_kernel(at_ref, x_hbm, cot_hbm, *refs):
    blocks, refs = refs[:9], refs[9:]
    both_ref, *outside, weights, x_ref, qkv_ref, probs_ref, context_ref, sems, more = refs
    tokens = fetch([(x_hbm, x_ref)], more)
    groups = load_weights(at_ref, blocks, weights, sems, (0, 1))
    cotangent = pltpu.make_async_copy(cot_hbm, both_ref.at[:, pl.ds(D, D)], more.at[1])
    cotangent.start()
    wait_all(tokens)
    x = x_ref[...].astype(F32)
    q, k, v = project(
        normalize(x)[0], weights, lambda: wait_all(groups[0]), lambda: wait_all(groups[1])
    )
    qkv_ref[0], qkv_ref[1], qkv_ref[2] = q, k, v
    left, right = out_weights(weights, 0), out_weights(weights, 1)
    context = attend(q, k, v, None, probs_ref)
    context_ref[...] = context
    copies = fetch(zip((qkv_ref, probs_ref, context_ref), outside), sems)
    both_ref[:, :D] = (x + project_out(context, left, right)).astype(BF)
    cotangent.wait()
    wait_all(copies)


def temporal_kernel(at_ref, both_hbm, order_hbm, *refs):
    back_ref, keep_ref, send_ref, weights, both_ref, order_ref, probs, sems, more = refs[9:]
    tokens, order = fetch([(both_hbm, both_ref), (order_hbm, order_ref)], more)
    groups = load_weights(at_ref, refs[:9], weights, sems, (0, 1))
    tokens.wait()
    hidden = both_ref[:, :D].astype(F32)
    normed, inverse = normalize(hidden)
    q, k, v = project(
        normed, weights, lambda: wait_all(groups[0]), lambda: wait_all(groups[1])
    )
    left, right = out_weights(weights, 0), out_weights(weights, 1)
    rows = lax.broadcasted_iota(jnp.int32, (TOKENS, TOKENS), 0)
    cols = lax.broadcasted_iota(jnp.int32, (TOKENS, TOKENS), 1)
    allowed = (rows & (PATCH_BLOCK - 1)) == (cols & (PATCH_BLOCK - 1))
    context = attend(q, k, v, allowed, probs)
    cot = both_ref[:, D:]
    order.wait()
    share = tn(nn(context, order_ref[...]).astype(BF), cot).astype(BF)
    keep_ref[...], send_ref[...] = share[:SHARE], share[SHARE:WIDTH]
    back_ref[:, D:] = (hidden + project_out(context, left, right)).astype(BF)
    cot = cot.astype(F32)
    context_grad = back_project_out(cot, left, right)
    dq, dk, dv = attend_back(q, k, v, context, context_grad, probs)
    normed_grad = rounded(back_project(dq, dk, dv, weights))
    back_ref[:, :D] = (cot + norm_back(normed_grad, normed, inverse)).astype(BF)


def backward_kernel(at_ref, x_hbm, both_hbm, qkv_hbm, probs_hbm, context_hbm, *refs):
    blocks, refs = refs[:9], refs[9:]
    input_grad_ref, weights, x_ref, grad_ref, qkv_ref, probs_ref, context_ref, sems, more = refs
    copies = fetch([(both_hbm.at[:, pl.ds(0, D)], grad_ref), (x_hbm, x_ref)], more)
    groups = load_weights(at_ref, blocks, weights, sems, (1, 0))
    kept = (qkv_hbm, qkv_ref), (probs_hbm, probs_ref), (context_hbm, context_ref)
    copies += [pltpu.make_async_copy(a, b, more.at[2 + n]) for n, (a, b) in enumerate(kept)]
    start_all(copies[2:])
    wait_all(copies[:2])
    grad = grad_ref[...].astype(F32)
    normed, inverse = normalize(x_ref[...].astype(F32))
    wait_all(groups[1])
    context_grad = back_project_out(grad, out_weights(weights, 0), out_weights(weights, 1))
    wait_all(copies[2:])
    dq, dk, dv = attend_back(
        qkv_ref[0], qkv_ref[1], qkv_ref[2], context_ref[...], context_grad, probs_ref
    )
    wait_all(groups[0])
    normed_grad = back_project(dq, dk, dv, weights)
    input_grad_ref[...] = (grad + norm_back(normed_grad, normed, inverse)).astype(BF)


def call(kernel, outs, scratch, micros, *args, smem=True, hbm=(), hbm_outs=()):
    in_specs = []
    for at in range(len(args)):
        space = pltpu.VMEM
        if smem and at == 0:
            space = pltpu.SMEM
        elif at in hbm:
            space = pl.ANY
        in_specs.append(pl.BlockSpec(memory_space=space))
    return pl.pallas_call(
        kernel,
        out_shape=[jax.ShapeDtypeStruct(s, t) for s, t in outs],
        in_specs=in_specs,
        out_specs=[
            pl.BlockSpec(memory_space=pl.ANY if n in hbm_outs else pltpu.VMEM)
            for n in range(len(outs))
        ],
        scratch_shapes=scratch,
        compiler_params=pltpu.CompilerParams(vmem_limit_bytes=VMEM_LIMIT),
        cost_estimate=pl.CostEstimate(
            flops=micros * 1_100_000_000, bytes_accessed=3_000_000, transcendentals=0
        ),
    )(*args)


def share_order(y, core):
    f = jnp.arange(PAD)
    dp, row = f // 18, f % 18
    half = row // 9
    far = jnp.where((dp // 4 - y) % 2 == 0, 0, 144) + jnp.where(half == core, 0, SHARE)
    at = far + dp // 8 * 36 + dp % 4 * 9 + row % 9
    at = jnp.where(f < WIDTH, at, -1)
    return (at[:, None] == jnp.arange(PAD)[None, :]).astype(BF)


GROUPS_FAR = [[y * 4 + z for y in range(p, 8, 2) for z in range(4)] for p in range(2)]
SWAP = [(s, s ^ 1) for s in range(16)]


def spread(block, axis, groups):
    count = len(groups[0])
    return lax.all_to_all(
        jnp.broadcast_to(block[None], (count,) + block.shape), axis, 0, 0,
        axis_index_groups=groups, tiled=True,
    )


def along_z(distance):
    pairs = []
    for y in range(8):
        for z in range(4):
            for s in range(16):
                to = (z + (distance if s % 2 == 0 else -distance)) % 4
                pairs.append(((y * 4 + z) * 16 + s, (y * 4 + to) * 16 + s))
    return pairs


def along_y(distance):
    pairs = []
    for y in range(8):
        for z in range(4):
            for s in range(16):
                to = (y + (distance if s % 2 == 0 else -distance)) % 8
                pairs.append(((y * 4 + z) * 16 + s, (to * 4 + z) * 16 + s))
    return pairs


UP = along_y(1)


def move(a, pairs):
    return lax.ppermute(a, ("dp", "seq"), pairs)


def per_device(clips, qkv_spatial, out_spatial, qkv_temporal, out_temporal, cotangent):
    x = clips.reshape(TOKENS, D)
    out_grad = cotangent.reshape(TOKENS, D)
    seq, dp = lax.axis_index("seq"), lax.axis_index("dp")
    y, chip, core = dp // 4, seq // 2, seq % 2
    at = jnp.stack([y, core, chip, dp % 4]).astype(jnp.int32)

    tokens_b = ((TOKENS, D), BF)
    wide_b = ((TOKENS, 2 * D), BF)
    probs = (HEADS, TOKENS, TOKENS)
    sems = pltpu.SemaphoreType.DMA((16,))

    def turn(a):
        parts = a.reshape(16, PATCH_BLOCK, 2 * D)
        return lax.all_to_all(parts, "seq", 0, 0, tiled=True).reshape(TOKENS, 2 * D)

    packed, packed_h, packed_t, packed_th = call(
        pack_kernel, [((72, D), BF), ((36, D), BF)] * 2,
        [
            pltpu.VMEM((3, 36, WIDTH), BF), pltpu.VMEM((18, D), BF),
            pltpu.VMEM((3, 36, WIDTH), BF), pltpu.VMEM((18, D), BF), sems,
        ],
        2, at, qkv_spatial, out_spatial, qkv_temporal, out_temporal, hbm=range(1, 5),
    )

    def swap(a):
        return lax.ppermute(a, "seq", SWAP)

    def column(rows, near, far):
        return call(
            column_kernel, [((2 * BLOCK, D), BF)], [], 2,
            at, rows, near, far, swap(jnp.concatenate([near, far])),
        )[0]

    def onward(ring):
        ring.append(move(ring[-1], UP))
        theirs = swap(ring[-2])
        ring[-1], theirs = lax.optimization_barrier((ring[-1], theirs))
        return theirs

    def final(ring):
        theirs = swap(ring[3])
        last = move(lax.dynamic_slice_in_dim(ring[3], core * BLOCK, BLOCK, axis=0), UP)
        return lax.optimization_barrier((last, theirs))

    near, far = move(packed, along_z(1)), move(packed_h, along_z(2))
    near, far, packed_t, packed_th = lax.optimization_barrier((near, far, packed_t, packed_th))
    near_t, far_t = move(packed_t, along_z(1)), move(packed_th, along_z(2))
    wgrad_order = share_order(y, core)

    block = column(packed, near, far)
    ring = [block, move(block, UP)]
    ring[1], near_t, far_t, wgrad_order = lax.optimization_barrier(
        (ring[1], near_t, far_t, wgrad_order)
    )
    block_t = column(packed_t, near_t, far_t)
    theirs = [onward(ring)]
    ring[2], block_t = lax.optimization_barrier((ring[2], block_t))
    ring_t = [block_t, move(block_t, UP)]
    theirs.append(onward(ring))
    last, other = final(ring)
    theirs_t = [onward(ring_t)]
    last_other, ring_t[2] = lax.optimization_barrier((swap(last), ring_t[2]))
    blocks = [*ring, *theirs, other, last, last_other]
    theirs_t.append(onward(ring_t))
    last_t, other = final(ring_t)
    blocks_t = [*ring_t, *theirs_t, other, last_t, swap(last_t)]

    more = pltpu.SemaphoreType.DMA((5,))
    weights = pltpu.VMEM((2 * D, D), BF)
    tokens, wide = pltpu.VMEM((TOKENS, D), BF), pltpu.VMEM((TOKENS, 2 * D), BF)
    kept = pltpu.VMEM((3, TOKENS, PAD), BF), pltpu.VMEM(probs, F32), pltpu.VMEM((TOKENS, PAD), BF)
    both, qkv, probs_s, context_s = call(
        forward_kernel,
        [wide_b, ((3, TOKENS, PAD), BF), (probs, F32), ((TOKENS, PAD), BF)],
        [weights, tokens, *kept, sems, more],
        8,
        at, x, out_grad, *blocks,
        hbm=range(1, 12), hbm_outs=(1, 2, 3),
    )
    both = turn(both)
    both_back, keep, send = call(
        temporal_kernel,
        [wide_b, ((SHARE, D), BF), ((SHARE, D), BF)],
        [weights, wide, pltpu.VMEM((PAD, PAD), BF), pltpu.VMEM(probs, F32), sems, more],
        12,
        at, both, wgrad_order, *blocks_t,
        hbm=range(1, 12),
    )
    both_back = turn(both_back)

    def add(a, b):
        return (a.astype(F32) + b.astype(F32)).astype(BF)

    total = add(keep, swap(send))
    total = add(total[:144], move(total[144:], UP))
    (input_grad,) = call(
        backward_kernel,
        [tokens_b],
        [weights, tokens, tokens, *kept, sems, more],
        9,
        at, x, both_back, qkv, probs_s, context_s, *blocks,
        hbm=range(1, 15),
    )
    over_z = lax.all_to_all(
        total.reshape(16, 9, D), "dp", 0, 0, axis_index_groups=GROUPS_FAR, tiled=True
    )
    over_z = jnp.sum(over_z.astype(F32), axis=0).astype(BF)
    over_z, input_grad = lax.optimization_barrier((over_z, input_grad))
    over_seq = spread(over_z, "seq", [list(range(16))]).reshape(8, 2, 9, D)
    out_temporal_grad = jnp.sum(over_seq.astype(F32), axis=0).reshape(18, D)
    mixed = both_back[:, D:]

    return mixed[None, None], input_grad[None, None], out_temporal_grad


def solution(mesh):
    tokens = P("dp", "seq", None, None)
    placed = (tokens, P(None, "dp", None), P("dp", None), P(None, "dp", None), P("dp", None), tokens)
    return jax.shard_map(
        per_device,
        mesh=mesh,
        in_specs=placed,
        out_specs=(tokens, tokens, P("dp", None)),
        check_vma=False,
    )
```

```python
import jax
import jax.numpy as jnp
from jax import lax
from jax.experimental import pallas as pl
from jax.experimental.pallas import tpu as pltpu
from jax.sharding import PartitionSpec as P

BF = jnp.bfloat16
F32 = jnp.float32
EPSILON = 1e-06
D = 1152
WIDTH = 576
PAD = 640
HEADS = 8
HEAD = 72
TOKENS = 128
PATCH_BLOCK = 8
SCALING = HEAD ** (-0.5)
SHARE = 288
BLOCK = 144
VMEM_LIMIT = 62 * 1024 * 1024


def nn(a, b):
    return lax.dot_general(a, b, (((1,), (0,)), ((), ())), preferred_element_type=F32)


def nt(a, b):
    return lax.dot_general(a, b, (((1,), (1,)), ((), ())), preferred_element_type=F32)


def tn(a, b):
    return lax.dot_general(a, b, (((0,), (0,)), ((), ())), preferred_element_type=F32)


def lanes(shape):
    return lax.broadcasted_iota(jnp.int32, shape, len(shape) - 1)


def normalize(values):
    centred = values - jnp.mean(values, axis=-1, keepdims=True)
    inverse = lax.rsqrt(jnp.mean(centred * centred, axis=-1, keepdims=True) + EPSILON)
    return centred * inverse, inverse


def norm_back(grad, normed, inverse):
    return inverse * (
        grad
        - jnp.mean(grad, axis=-1, keepdims=True)
        - normed * jnp.mean(grad * normed, axis=-1, keepdims=True)
    )


def keep_width(a):
    return jnp.where(lanes(a.shape) < WIDTH, a, 0.0)


def window(h):
    low = h * HEAD // 128 * 128
    high = -(-(h * HEAD + HEAD) // 128) * 128
    return low, high


def head_mask(h):
    low, high = window(h)
    at = lanes((TOKENS, high - low)) + low
    return (at >= h * HEAD) & (at < h * HEAD + HEAD)


def add_window(tiles, h, part):
    low, high = window(h)
    part = jnp.where(head_mask(h), part, 0.0)
    for t in range(low // 128, high // 128):
        piece = part[:, t * 128 - low : t * 128 - low + 128]
        tiles[t] = piece if tiles[t] is None else tiles[t] + piece


def join(tiles):
    return jnp.concatenate(tiles, axis=1)


def rounded(a):
    return a.astype(BF).astype(F32)


def attend(q, k, v, allowed, probs_ref):
    tiles = [None] * (PAD // 128)
    for h in range(HEADS):
        low, high = window(h)
        masked = jnp.where(head_mask(h), q[:, low:high].astype(F32), 0.0).astype(BF)
        scores = nt(masked, k[:, low:high]) * SCALING
        if allowed is not None:
            scores = jnp.where(allowed, scores, -1e38)
        powers = jnp.exp(scores - jnp.max(scores, axis=-1, keepdims=True))
        probs = powers / jnp.sum(powers, axis=-1, keepdims=True)
        probs_ref[h] = probs
        add_window(tiles, h, nn(probs.astype(BF), v[:, low:high]))
    return join(tiles).astype(BF)


def attend_back(q, k, v, context, context_grad, probs_ref):
    dq, dk, dv = ([None] * (PAD // 128) for _ in range(3))
    for h in range(HEADS):
        low, high = window(h)
        grad = context_grad[:, low:high]
        masked = jnp.where(head_mask(h), grad.astype(F32), 0.0)
        probs = probs_ref[h]
        prob_grad = nt(masked.astype(BF), v[:, low:high])
        row = jnp.sum(masked * context[:, low:high].astype(F32), axis=-1, keepdims=True)
        score_grad = (probs * (prob_grad - row) * SCALING).astype(BF)
        add_window(dv, h, tn(probs.astype(BF), grad))
        add_window(dq, h, nn(score_grad, k[:, low:high]))
        add_window(dk, h, tn(score_grad, q[:, low:high]))
    return rounded(join(dq)), rounded(join(dk)), rounded(join(dv))


def start_all(copies):
    for copy in copies:
        copy.start()
    return copies


def wait_all(copies):
    for copy in copies:
        copy.wait()


def load_weights(at_ref, blocks, weights, sems, order):
    y, core = at_ref[0], at_ref[1]
    sign = 1 - 2 * core

    def copy(source, half, place, sem):
        at = pl.multiple_of(half * D + lax.rem(place + 16, 8) * BLOCK, BLOCK)
        return pltpu.make_async_copy(source, weights.at[pl.ds(at, BLOCK), :], sems.at[sem])

    last = start_all([copy(blocks[7], core, y + 4, 0), copy(blocks[8], 1 - core, y + 4, 8)])
    groups = {}
    for half in order:
        rows = pl.ds(half * BLOCK, BLOCK)
        copies = [copy(blocks[0].at[rows, :], half, y, half * 8 + 1)]
        for step in range(1, 4):
            below, above = blocks[step].at[rows, :], blocks[3 + step].at[rows, :]
            copies.append(copy(below, half, y - sign * step, half * 8 + 2 * step))
            copies.append(copy(above, half, y + sign * step, half * 8 + 2 * step + 1))
        groups[half] = start_all(copies)
    groups[order[0]] = last + groups[order[0]]
    return groups


def project(normed, weights, wait_first, wait_second):
    normed_b = normed.astype(BF)
    wait_first()
    qk = nn(normed_b, weights[:D, :])
    wait_second()
    v = keep_width(nn(normed_b, weights[D:, :PAD]))
    k = pltpu.roll(qk, WIDTH, 1)
    return qk[:, :PAD].astype(BF), k[:, :PAD].astype(BF), v.astype(BF)


def pair_lanes(dq, dk):
    zeros = jnp.zeros((TOKENS, D - PAD), F32)
    return jnp.concatenate([dq, zeros], axis=1) + pltpu.roll(
        jnp.concatenate([dk, zeros], axis=1), WIDTH, 1
    )


def back_project(dq, dk, dv, weights):
    return nt(pair_lanes(dq, dk).astype(BF), weights[:D, :]) + nt(dv.astype(BF), weights[D:, :PAD])


def late(a):
    return jnp.where(lanes(a.shape) >= PAD - WIDTH, a, 0.0)


def out_weights(weights, side):
    starts = [D + y * BLOCK + side * 72 for y in range(8)]
    return jnp.concatenate([weights[at : at + 72, D - PAD :] for at in starts], axis=0)


def project_out(context, left, right):
    zeros = jnp.zeros((TOKENS, D - PAD), F32)
    context = context[:, :WIDTH]
    first, second = late(nn(context, left)), late(nn(context, right))
    return pltpu.roll(
        jnp.concatenate([first, zeros], axis=1), D - (PAD - WIDTH), 1
    ) + jnp.concatenate([zeros, second], axis=1)


def back_project_out(grad, left, right):
    first = late(pltpu.roll(grad, PAD - WIDTH, 1)[:, :PAD])
    second = late(grad[:, D - PAD :])
    context_grad = nt(first.astype(BF), left) + nt(second.astype(BF), right)
    return jnp.concatenate([context_grad, jnp.zeros((TOKENS, PAD - WIDTH), F32)], axis=1).astype(BF)


def selection(rows, columns, shift):
    r = lax.broadcasted_iota(jnp.int32, (rows, columns), 0)
    c = lax.broadcasted_iota(jnp.int32, (rows, columns), 1)
    return r + shift == c


def pack_kernel(at_ref, *refs):
    outside, inside_refs, sems = refs[:4], refs[8:12], refs[12]
    wait_all(
        start_all(
            [
                pltpu.make_async_copy(a, b, sems.at[n])
                for n, (a, b) in enumerate(zip(outside, inside_refs))
            ]
        )
    )
    qkv_s, out_s, qkv_t, out_t = inside_refs
    core = at_ref[1]

    def pick(which, a):
        return nn(which.astype(F32).astype(BF), a)

    def side(a, b):
        return jnp.concatenate([a, b], axis=1)

    lead = selection(36, 18, 0)
    tail = selection(36, 18, -18)

    def blocks(qkv, out_ref):
        q, k, v, out = qkv[0], qkv[1], qkv[2], out_ref[...]
        halves = pick(lead, out[:, :WIDTH]) + pick(tail, out[:, WIDTH:])
        return side(q.astype(F32), k.astype(F32)), side(v.astype(F32), halves)

    for n, (qkv, out_ref) in enumerate(((qkv_s, out_s), (qkv_t, out_t))):
        all_ref, half_ref = refs[4 + 2 * n : 6 + 2 * n]
        first, second = blocks(qkv, out_ref)
        half_ref[...] = jnp.where(core == 0, first, second).astype(BF)
        all_ref[...] = jnp.concatenate([first, second], axis=0).astype(BF)


def in_sides(parts):
    plain = jnp.concatenate(parts, axis=0)
    by_side = jnp.concatenate([p[:18] for p in parts] + [p[18:] for p in parts], axis=0)
    return jnp.where(lanes(plain.shape) < WIDTH, plain, by_side)


def in_order(z, own, below, above, far):
    parts = []
    for place in range(4):
        distance = lax.rem(place - z + 4, 4)
        part = jnp.where(distance == 0, own, jnp.where(distance == 1, above, far))
        parts.append(jnp.where(distance == 3, below, part))
    return parts


def column_kernel(at_ref, own_ref, next_ref, far_ref, other_ref, block_ref):
    z, core = at_ref[3], at_ref[1]
    own, near, far = (ref[...].astype(F32) for ref in (own_ref, next_ref, far_ref))
    other = other_ref[...].astype(F32)
    below = jnp.where(core == 0, near, other[:72])
    above = jnp.where(core == 0, other[:72], near)
    low = jnp.where(core == 0, far, other[72:])
    high = jnp.where(core == 0, other[72:], far)
    first = in_order(z, own[:36], below[:36], above[:36], low)
    second = in_order(z, own[36:], below[36:], above[36:], high)
    block_ref[:BLOCK] = jnp.concatenate(first, axis=0).astype(BF)
    block_ref[BLOCK:] = in_sides(second).astype(BF)


def fetch(pairs, sems):
    return start_all(
        [pltpu.make_async_copy(a, b, sems.at[n]) for n, (a, b) in enumerate(pairs)]
    )


def forward_kernel(at_ref, x_hbm, cot_hbm, *refs):
    blocks, refs = refs[:9], refs[9:]
    both_ref, *outside, weights, x_ref, qkv_ref, probs_ref, context_ref, sems, more = refs
    tokens = fetch([(x_hbm, x_ref)], more)
    groups = load_weights(at_ref, blocks, weights, sems, (0, 1))
    cotangent = pltpu.make_async_copy(cot_hbm, both_ref.at[:, pl.ds(D, D)], more.at[1])
    cotangent.start()
    wait_all(tokens)
    x = x_ref[...].astype(F32)
    q, k, v = project(
        normalize(x)[0], weights, lambda: wait_all(groups[0]), lambda: wait_all(groups[1])
    )
    qkv_ref[0], qkv_ref[1], qkv_ref[2] = q, k, v
    left, right = out_weights(weights, 0), out_weights(weights, 1)
    context = attend(q, k, v, None, probs_ref)
    context_ref[...] = context
    copies = fetch(zip((qkv_ref, probs_ref, context_ref), outside), sems)
    both_ref[:, :D] = (x + project_out(context, left, right)).astype(BF)
    cotangent.wait()
    wait_all(copies)


def temporal_kernel(at_ref, both_hbm, order_hbm, *refs):
    back_ref, keep_ref, send_ref, weights, both_ref, order_ref, probs, sems, more = refs[9:]
    tokens, order = fetch([(both_hbm, both_ref), (order_hbm, order_ref)], more)
    groups = load_weights(at_ref, refs[:9], weights, sems, (0, 1))
    tokens.wait()
    hidden = both_ref[:, :D].astype(F32)
    normed, inverse = normalize(hidden)
    q, k, v = project(
        normed, weights, lambda: wait_all(groups[0]), lambda: wait_all(groups[1])
    )
    left, right = out_weights(weights, 0), out_weights(weights, 1)
    rows = lax.broadcasted_iota(jnp.int32, (TOKENS, TOKENS), 0)
    cols = lax.broadcasted_iota(jnp.int32, (TOKENS, TOKENS), 1)
    allowed = (rows & (PATCH_BLOCK - 1)) == (cols & (PATCH_BLOCK - 1))
    context = attend(q, k, v, allowed, probs)
    cot = both_ref[:, D:]
    order.wait()
    share = tn(nn(context, order_ref[...]).astype(BF), cot).astype(BF)
    keep_ref[...], send_ref[...] = share[:SHARE], share[SHARE:WIDTH]
    back_ref[:, D:] = (hidden + project_out(context, left, right)).astype(BF)
    cot = cot.astype(F32)
    context_grad = back_project_out(cot, left, right)
    dq, dk, dv = attend_back(q, k, v, context, context_grad, probs)
    normed_grad = rounded(back_project(dq, dk, dv, weights))
    back_ref[:, :D] = (cot + norm_back(normed_grad, normed, inverse)).astype(BF)


def backward_kernel(at_ref, x_hbm, both_hbm, qkv_hbm, probs_hbm, context_hbm, *refs):
    blocks, refs = refs[:9], refs[9:]
    input_grad_ref, weights, x_ref, grad_ref, qkv_ref, probs_ref, context_ref, sems, more = refs
    copies = fetch([(both_hbm.at[:, pl.ds(0, D)], grad_ref), (x_hbm, x_ref)], more)
    groups = load_weights(at_ref, blocks, weights, sems, (1, 0))
    kept = (qkv_hbm, qkv_ref), (probs_hbm, probs_ref), (context_hbm, context_ref)
    copies += [pltpu.make_async_copy(a, b, more.at[2 + n]) for n, (a, b) in enumerate(kept)]
    start_all(copies[2:])
    wait_all(copies[:2])
    grad = grad_ref[...].astype(F32)
    normed, inverse = normalize(x_ref[...].astype(F32))
    wait_all(groups[1])
    context_grad = back_project_out(grad, out_weights(weights, 0), out_weights(weights, 1))
    wait_all(copies[2:])
    dq, dk, dv = attend_back(
        qkv_ref[0], qkv_ref[1], qkv_ref[2], context_ref[...], context_grad, probs_ref
    )
    wait_all(groups[0])
    normed_grad = back_project(dq, dk, dv, weights)
    input_grad_ref[...] = (grad + norm_back(normed_grad, normed, inverse)).astype(BF)


def call(kernel, outs, scratch, micros, *args, smem=True, hbm=(), hbm_outs=()):
    in_specs = []
    for at in range(len(args)):
        space = pltpu.VMEM
        if smem and at == 0:
            space = pltpu.SMEM
        elif at in hbm:
            space = pl.ANY
        in_specs.append(pl.BlockSpec(memory_space=space))
    return pl.pallas_call(
        kernel,
        out_shape=[jax.ShapeDtypeStruct(s, t) for s, t in outs],
        in_specs=in_specs,
        out_specs=[
            pl.BlockSpec(memory_space=pl.ANY if n in hbm_outs else pltpu.VMEM)
            for n in range(len(outs))
        ],
        scratch_shapes=scratch,
        compiler_params=pltpu.CompilerParams(vmem_limit_bytes=VMEM_LIMIT),
        cost_estimate=pl.CostEstimate(
            flops=micros * 1_100_000_000, bytes_accessed=3_000_000, transcendentals=0
        ),
    )(*args)


def share_order(y, core):
    f = jnp.arange(PAD)
    dp, row = f // 18, f % 18
    half = row // 9
    far = jnp.where((dp // 4 - y) % 2 == 0, 0, 144) + jnp.where(half == core, 0, SHARE)
    at = far + dp // 8 * 36 + dp % 4 * 9 + row % 9
    at = jnp.where(f < WIDTH, at, -1)
    return (at[:, None] == jnp.arange(PAD)[None, :]).astype(BF)


GROUPS_FAR = [[y * 4 + z for y in range(p, 8, 2) for z in range(4)] for p in range(2)]
SWAP = [(s, s ^ 1) for s in range(16)]


def spread(block, axis, groups):
    count = len(groups[0])
    return lax.all_to_all(
        jnp.broadcast_to(block[None], (count,) + block.shape), axis, 0, 0,
        axis_index_groups=groups, tiled=True,
    )


def along_z(distance):
    pairs = []
    for y in range(8):
        for z in range(4):
            for s in range(16):
                to = (z + (distance if s % 2 == 0 else -distance)) % 4
                pairs.append(((y * 4 + z) * 16 + s, (y * 4 + to) * 16 + s))
    return pairs


def along_y(distance):
    pairs = []
    for y in range(8):
        for z in range(4):
            for s in range(16):
                to = (y + (distance if s % 2 == 0 else -distance)) % 8
                pairs.append(((y * 4 + z) * 16 + s, (to * 4 + z) * 16 + s))
    return pairs


UP = along_y(1)


def move(a, pairs):
    return lax.ppermute(a, ("dp", "seq"), pairs)


def per_device(clips, qkv_spatial, out_spatial, qkv_temporal, out_temporal, cotangent):
    x = clips.reshape(TOKENS, D)
    out_grad = cotangent.reshape(TOKENS, D)
    seq, dp = lax.axis_index("seq"), lax.axis_index("dp")
    y, chip, core = dp // 4, seq // 2, seq % 2
    at = jnp.stack([y, core, chip, dp % 4]).astype(jnp.int32)

    tokens_b = ((TOKENS, D), BF)
    wide_b = ((TOKENS, 2 * D), BF)
    probs = (HEADS, TOKENS, TOKENS)
    sems = pltpu.SemaphoreType.DMA((16,))

    def turn(a):
        parts = a.reshape(16, PATCH_BLOCK, 2 * D)
        return lax.all_to_all(parts, "seq", 0, 0, tiled=True).reshape(TOKENS, 2 * D)

    packed, packed_h, packed_t, packed_th = call(
        pack_kernel, [((72, D), BF), ((36, D), BF)] * 2,
        [
            pltpu.VMEM((3, 36, WIDTH), BF), pltpu.VMEM((18, D), BF),
            pltpu.VMEM((3, 36, WIDTH), BF), pltpu.VMEM((18, D), BF), sems,
        ],
        2, at, qkv_spatial, out_spatial, qkv_temporal, out_temporal, hbm=range(1, 5),
    )

    def swap(a):
        return lax.ppermute(a, "seq", SWAP)

    def column(rows, near, far):
        return call(
            column_kernel, [((2 * BLOCK, D), BF)], [], 2,
            at, rows, near, far, swap(jnp.concatenate([near, far])),
        )[0]

    def onward(ring):
        ring.append(move(ring[-1], UP))
        theirs = swap(ring[-2])
        ring[-1], theirs = lax.optimization_barrier((ring[-1], theirs))
        return theirs

    def final(ring):
        theirs = swap(ring[3])
        last = move(lax.dynamic_slice_in_dim(ring[3], core * BLOCK, BLOCK, axis=0), UP)
        return lax.optimization_barrier((last, theirs))

    near, far = move(packed, along_z(1)), move(packed_h, along_z(2))
    near, far, packed_t, packed_th = lax.optimization_barrier((near, far, packed_t, packed_th))
    near_t, far_t = move(packed_t, along_z(1)), move(packed_th, along_z(2))
    wgrad_order = share_order(y, core)

    block = column(packed, near, far)
    ring = [block, move(block, UP)]
    ring[1], wgrad_order = lax.optimization_barrier((ring[1], wgrad_order))
    block_t = column(packed_t, near_t, far_t)
    theirs = [onward(ring)]
    ring[2], block_t = lax.optimization_barrier((ring[2], block_t))
    ring_t = [block_t, move(block_t, UP)]
    theirs.append(onward(ring))
    last, other = final(ring)
    theirs_t = [onward(ring_t)]
    last_other, ring_t[2] = lax.optimization_barrier((swap(last), ring_t[2]))
    blocks = [*ring, *theirs, other, last, last_other]
    theirs_t.append(onward(ring_t))
    last_t, other = final(ring_t)
    blocks_t = [*ring_t, *theirs_t, other, last_t, swap(last_t)]

    more = pltpu.SemaphoreType.DMA((5,))
    weights = pltpu.VMEM((2 * D, D), BF)
    tokens, wide = pltpu.VMEM((TOKENS, D), BF), pltpu.VMEM((TOKENS, 2 * D), BF)
    kept = pltpu.VMEM((3, TOKENS, PAD), BF), pltpu.VMEM(probs, F32), pltpu.VMEM((TOKENS, PAD), BF)
    both, qkv, probs_s, context_s = call(
        forward_kernel,
        [wide_b, ((3, TOKENS, PAD), BF), (probs, F32), ((TOKENS, PAD), BF)],
        [weights, tokens, *kept, sems, more],
        8,
        at, x, out_grad, *blocks,
        hbm=range(1, 12), hbm_outs=(1, 2, 3),
    )
    both = turn(both)
    both_back, keep, send = call(
        temporal_kernel,
        [wide_b, ((SHARE, D), BF), ((SHARE, D), BF)],
        [weights, wide, pltpu.VMEM((PAD, PAD), BF), pltpu.VMEM(probs, F32), sems, more],
        12,
        at, both, wgrad_order, *blocks_t,
        hbm=range(1, 12),
    )
    both_back = turn(both_back)

    def add(a, b):
        return (a.astype(F32) + b.astype(F32)).astype(BF)

    total = add(keep, swap(send))
    total = add(total[:144], move(total[144:], UP))
    (input_grad,) = call(
        backward_kernel,
        [tokens_b],
        [weights, tokens, tokens, *kept, sems, more],
        9,
        at, x, both_back, qkv, probs_s, context_s, *blocks,
        hbm=range(1, 15),
    )
    over_z = lax.all_to_all(
        total.reshape(16, 9, D), "dp", 0, 0, axis_index_groups=GROUPS_FAR, tiled=True
    )
    over_z = jnp.sum(over_z.astype(F32), axis=0).astype(BF)
    over_z, input_grad = lax.optimization_barrier((over_z, input_grad))
    over_seq = spread(over_z, "seq", [list(range(16))]).reshape(8, 2, 9, D)
    out_temporal_grad = jnp.sum(over_seq.astype(F32), axis=0).reshape(18, D)
    mixed = both_back[:, D:]

    return mixed[None, None], input_grad[None, None], out_temporal_grad


def solution(mesh):
    tokens = P("dp", "seq", None, None)
    placed = (tokens, P(None, "dp", None), P("dp", None), P(None, "dp", None), P("dp", None), tokens)
    return jax.shard_map(
        per_device,
        mesh=mesh,
        in_specs=placed,
        out_specs=(tokens, tokens, P("dp", None)),
        check_vma=False,
    )
```

```python
import jax
import jax.numpy as jnp
from jax import lax
from jax.experimental import pallas as pl
from jax.experimental.pallas import tpu as pltpu
from jax.sharding import PartitionSpec as P

BF = jnp.bfloat16
F32 = jnp.float32
EPSILON = 1e-06
D = 1152
WIDTH = 576
PAD = 640
HEADS = 8
HEAD = 72
TOKENS = 128
PATCH_BLOCK = 8
SCALING = HEAD ** (-0.5)
SHARE = 288
BLOCK = 144
VMEM_LIMIT = 62 * 1024 * 1024


def nn(a, b):
    return lax.dot_general(a, b, (((1,), (0,)), ((), ())), preferred_element_type=F32)


def nt(a, b):
    return lax.dot_general(a, b, (((1,), (1,)), ((), ())), preferred_element_type=F32)


def tn(a, b):
    return lax.dot_general(a, b, (((0,), (0,)), ((), ())), preferred_element_type=F32)


def lanes(shape):
    return lax.broadcasted_iota(jnp.int32, shape, len(shape) - 1)


def normalize(values):
    centred = values - jnp.mean(values, axis=-1, keepdims=True)
    inverse = lax.rsqrt(jnp.mean(centred * centred, axis=-1, keepdims=True) + EPSILON)
    return centred * inverse, inverse


def norm_back(grad, normed, inverse):
    return inverse * (
        grad
        - jnp.mean(grad, axis=-1, keepdims=True)
        - normed * jnp.mean(grad * normed, axis=-1, keepdims=True)
    )


def keep_width(a):
    return jnp.where(lanes(a.shape) < WIDTH, a, 0.0)


def window(h):
    low = h * HEAD // 128 * 128
    high = -(-(h * HEAD + HEAD) // 128) * 128
    return low, high


def head_mask(h):
    low, high = window(h)
    at = lanes((TOKENS, high - low)) + low
    return (at >= h * HEAD) & (at < h * HEAD + HEAD)


def add_window(tiles, h, part):
    low, high = window(h)
    part = jnp.where(head_mask(h), part, 0.0)
    for t in range(low // 128, high // 128):
        piece = part[:, t * 128 - low : t * 128 - low + 128]
        tiles[t] = piece if tiles[t] is None else tiles[t] + piece


def join(tiles):
    return jnp.concatenate(tiles, axis=1)


def rounded(a):
    return a.astype(BF).astype(F32)


def attend(q, k, v, allowed, probs_ref):
    tiles = [None] * (PAD // 128)
    for h in range(HEADS):
        low, high = window(h)
        masked = jnp.where(head_mask(h), q[:, low:high].astype(F32), 0.0).astype(BF)
        scores = nt(masked, k[:, low:high]) * SCALING
        if allowed is not None:
            scores = jnp.where(allowed, scores, -1e38)
        powers = jnp.exp(scores - jnp.max(scores, axis=-1, keepdims=True))
        probs = powers / jnp.sum(powers, axis=-1, keepdims=True)
        probs_ref[h] = probs
        add_window(tiles, h, nn(probs.astype(BF), v[:, low:high]))
    return join(tiles).astype(BF)


def attend_back(q, k, v, context, context_grad, probs_ref):
    dq, dk, dv = ([None] * (PAD // 128) for _ in range(3))
    for h in range(HEADS):
        low, high = window(h)
        grad = context_grad[:, low:high]
        masked = jnp.where(head_mask(h), grad.astype(F32), 0.0)
        probs = probs_ref[h]
        prob_grad = nt(masked.astype(BF), v[:, low:high])
        row = jnp.sum(masked * context[:, low:high].astype(F32), axis=-1, keepdims=True)
        score_grad = (probs * (prob_grad - row) * SCALING).astype(BF)
        add_window(dv, h, tn(probs.astype(BF), grad))
        add_window(dq, h, nn(score_grad, k[:, low:high]))
        add_window(dk, h, tn(score_grad, q[:, low:high]))
    return rounded(join(dq)), rounded(join(dk)), rounded(join(dv))


def start_all(copies):
    for copy in copies:
        copy.start()
    return copies


def wait_all(copies):
    for copy in copies:
        copy.wait()


def load_weights(at_ref, blocks, weights, sems, order):
    y, core = at_ref[0], at_ref[1]
    sign = 1 - 2 * core

    def copy(source, half, place, sem):
        at = pl.multiple_of(half * D + lax.rem(place + 16, 8) * BLOCK, BLOCK)
        return pltpu.make_async_copy(source, weights.at[pl.ds(at, BLOCK), :], sems.at[sem])

    last = start_all([copy(blocks[7], core, y + 4, 0), copy(blocks[8], 1 - core, y + 4, 8)])
    groups = {}
    for half in order:
        rows = pl.ds(half * BLOCK, BLOCK)
        copies = [copy(blocks[0].at[rows, :], half, y, half * 8 + 1)]
        for step in range(1, 4):
            below, above = blocks[step].at[rows, :], blocks[3 + step].at[rows, :]
            copies.append(copy(below, half, y - sign * step, half * 8 + 2 * step))
            copies.append(copy(above, half, y + sign * step, half * 8 + 2 * step + 1))
        groups[half] = start_all(copies)
    groups[order[0]] = last + groups[order[0]]
    return groups


def project(normed, weights, wait_first, wait_second):
    normed_b = normed.astype(BF)
    wait_first()
    qk = nn(normed_b, weights[:D, :])
    wait_second()
    v = keep_width(nn(normed_b, weights[D:, :PAD]))
    k = pltpu.roll(qk, WIDTH, 1)
    return qk[:, :PAD].astype(BF), k[:, :PAD].astype(BF), v.astype(BF)


def pair_lanes(dq, dk):
    zeros = jnp.zeros((TOKENS, D - PAD), F32)
    return jnp.concatenate([dq, zeros], axis=1) + pltpu.roll(
        jnp.concatenate([dk, zeros], axis=1), WIDTH, 1
    )


def back_project(dq, dk, dv, weights):
    return nt(pair_lanes(dq, dk).astype(BF), weights[:D, :]) + nt(dv.astype(BF), weights[D:, :PAD])


def late(a):
    return jnp.where(lanes(a.shape) >= PAD - WIDTH, a, 0.0)


def out_weights(weights, side):
    starts = [D + y * BLOCK + side * 72 for y in range(8)]
    return jnp.concatenate([weights[at : at + 72, D - PAD :] for at in starts], axis=0)


def project_out(context, left, right):
    zeros = jnp.zeros((TOKENS, D - PAD), F32)
    context = context[:, :WIDTH]
    first, second = late(nn(context, left)), late(nn(context, right))
    return pltpu.roll(
        jnp.concatenate([first, zeros], axis=1), D - (PAD - WIDTH), 1
    ) + jnp.concatenate([zeros, second], axis=1)


def back_project_out(grad, left, right):
    first = late(pltpu.roll(grad, PAD - WIDTH, 1)[:, :PAD])
    second = late(grad[:, D - PAD :])
    context_grad = nt(first.astype(BF), left) + nt(second.astype(BF), right)
    return jnp.concatenate([context_grad, jnp.zeros((TOKENS, PAD - WIDTH), F32)], axis=1).astype(BF)


def selection(rows, columns, shift):
    r = lax.broadcasted_iota(jnp.int32, (rows, columns), 0)
    c = lax.broadcasted_iota(jnp.int32, (rows, columns), 1)
    return r + shift == c


def pack_kernel(at_ref, *refs):
    outside, inside_refs, sems = refs[:4], refs[8:12], refs[12]
    wait_all(
        start_all(
            [
                pltpu.make_async_copy(a, b, sems.at[n])
                for n, (a, b) in enumerate(zip(outside, inside_refs))
            ]
        )
    )
    qkv_s, out_s, qkv_t, out_t = inside_refs
    core = at_ref[1]

    def pick(which, a):
        return nn(which.astype(F32).astype(BF), a)

    def side(a, b):
        return jnp.concatenate([a, b], axis=1)

    lead = selection(36, 18, 0)
    tail = selection(36, 18, -18)

    def blocks(qkv, out_ref):
        q, k, v, out = qkv[0], qkv[1], qkv[2], out_ref[...]
        halves = pick(lead, out[:, :WIDTH]) + pick(tail, out[:, WIDTH:])
        return side(q.astype(F32), k.astype(F32)), side(v.astype(F32), halves)

    for n, (qkv, out_ref) in enumerate(((qkv_s, out_s), (qkv_t, out_t))):
        all_ref, half_ref = refs[4 + 2 * n : 6 + 2 * n]
        first, second = blocks(qkv, out_ref)
        half_ref[...] = jnp.where(core == 0, first, second).astype(BF)
        all_ref[...] = jnp.concatenate([first, second], axis=0).astype(BF)


def in_sides(parts):
    plain = jnp.concatenate(parts, axis=0)
    by_side = jnp.concatenate([p[:18] for p in parts] + [p[18:] for p in parts], axis=0)
    return jnp.where(lanes(plain.shape) < WIDTH, plain, by_side)


def in_order(z, own, below, above, far):
    parts = []
    for place in range(4):
        distance = lax.rem(place - z + 4, 4)
        part = jnp.where(distance == 0, own, jnp.where(distance == 1, above, far))
        parts.append(jnp.where(distance == 3, below, part))
    return parts


def column_kernel(at_ref, own_ref, next_ref, far_ref, other_ref, block_ref):
    z, core = at_ref[3], at_ref[1]
    own, near, far = (ref[...].astype(F32) for ref in (own_ref, next_ref, far_ref))
    other = other_ref[...].astype(F32)
    below = jnp.where(core == 0, near, other[:72])
    above = jnp.where(core == 0, other[:72], near)
    low = jnp.where(core == 0, far, other[72:])
    high = jnp.where(core == 0, other[72:], far)
    first = in_order(z, own[:36], below[:36], above[:36], low)
    second = in_order(z, own[36:], below[36:], above[36:], high)
    block_ref[:BLOCK] = jnp.concatenate(first, axis=0).astype(BF)
    block_ref[BLOCK:] = in_sides(second).astype(BF)


def fetch(pairs, sems):
    return start_all(
        [pltpu.make_async_copy(a, b, sems.at[n]) for n, (a, b) in enumerate(pairs)]
    )


def forward_kernel(at_ref, x_hbm, cot_hbm, *refs):
    blocks, refs = refs[:9], refs[9:]
    both_ref, *outside, weights, x_ref, qkv_ref, probs_ref, context_ref, sems, more = refs
    tokens = fetch([(x_hbm, x_ref)], more)
    groups = load_weights(at_ref, blocks, weights, sems, (0, 1))
    cotangent = pltpu.make_async_copy(cot_hbm, both_ref.at[:, pl.ds(D, D)], more.at[1])
    cotangent.start()
    wait_all(tokens)
    x = x_ref[...].astype(F32)
    q, k, v = project(
        normalize(x)[0], weights, lambda: wait_all(groups[0]), lambda: wait_all(groups[1])
    )
    qkv_ref[0], qkv_ref[1], qkv_ref[2] = q, k, v
    left, right = out_weights(weights, 0), out_weights(weights, 1)
    context = attend(q, k, v, None, probs_ref)
    context_ref[...] = context
    copies = fetch(zip((qkv_ref, probs_ref, context_ref), outside), sems)
    both_ref[:, :D] = (x + project_out(context, left, right)).astype(BF)
    cotangent.wait()
    wait_all(copies)


def temporal_kernel(at_ref, both_hbm, order_hbm, *refs):
    back_ref, keep_ref, send_ref, weights, both_ref, order_ref, probs, sems, more = refs[9:]
    tokens, order = fetch([(both_hbm, both_ref), (order_hbm, order_ref)], more)
    groups = load_weights(at_ref, refs[:9], weights, sems, (0, 1))
    tokens.wait()
    hidden = both_ref[:, :D].astype(F32)
    normed, inverse = normalize(hidden)
    q, k, v = project(
        normed, weights, lambda: wait_all(groups[0]), lambda: wait_all(groups[1])
    )
    left, right = out_weights(weights, 0), out_weights(weights, 1)
    rows = lax.broadcasted_iota(jnp.int32, (TOKENS, TOKENS), 0)
    cols = lax.broadcasted_iota(jnp.int32, (TOKENS, TOKENS), 1)
    allowed = (rows & (PATCH_BLOCK - 1)) == (cols & (PATCH_BLOCK - 1))
    context = attend(q, k, v, allowed, probs)
    cot = both_ref[:, D:]
    order.wait()
    share = tn(nn(context, order_ref[...]).astype(BF), cot).astype(BF)
    keep_ref[...], send_ref[...] = share[:SHARE], share[SHARE:WIDTH]
    back_ref[:, D:] = (hidden + project_out(context, left, right)).astype(BF)
    cot = cot.astype(F32)
    context_grad = back_project_out(cot, left, right)
    dq, dk, dv = attend_back(q, k, v, context, context_grad, probs)
    normed_grad = rounded(back_project(dq, dk, dv, weights))
    back_ref[:, :D] = (cot + norm_back(normed_grad, normed, inverse)).astype(BF)


def backward_kernel(at_ref, x_hbm, both_hbm, qkv_hbm, probs_hbm, context_hbm, *refs):
    blocks, refs = refs[:9], refs[9:]
    input_grad_ref, weights, x_ref, grad_ref, qkv_ref, probs_ref, context_ref, sems, more = refs
    copies = fetch([(both_hbm.at[:, pl.ds(0, D)], grad_ref), (x_hbm, x_ref)], more)
    groups = load_weights(at_ref, blocks, weights, sems, (1, 0))
    kept = (qkv_hbm, qkv_ref), (probs_hbm, probs_ref), (context_hbm, context_ref)
    copies += [pltpu.make_async_copy(a, b, more.at[2 + n]) for n, (a, b) in enumerate(kept)]
    start_all(copies[2:])
    wait_all(copies[:2])
    grad = grad_ref[...].astype(F32)
    normed, inverse = normalize(x_ref[...].astype(F32))
    wait_all(groups[1])
    context_grad = back_project_out(grad, out_weights(weights, 0), out_weights(weights, 1))
    wait_all(copies[2:])
    dq, dk, dv = attend_back(
        qkv_ref[0], qkv_ref[1], qkv_ref[2], context_ref[...], context_grad, probs_ref
    )
    wait_all(groups[0])
    normed_grad = back_project(dq, dk, dv, weights)
    input_grad_ref[...] = (grad + norm_back(normed_grad, normed, inverse)).astype(BF)


def call(kernel, outs, scratch, micros, *args, smem=True, hbm=(), hbm_outs=()):
    in_specs = []
    for at in range(len(args)):
        space = pltpu.VMEM
        if smem and at == 0:
            space = pltpu.SMEM
        elif at in hbm:
            space = pl.ANY
        in_specs.append(pl.BlockSpec(memory_space=space))
    return pl.pallas_call(
        kernel,
        out_shape=[jax.ShapeDtypeStruct(s, t) for s, t in outs],
        in_specs=in_specs,
        out_specs=[
            pl.BlockSpec(memory_space=pl.ANY if n in hbm_outs else pltpu.VMEM)
            for n in range(len(outs))
        ],
        scratch_shapes=scratch,
        compiler_params=pltpu.CompilerParams(vmem_limit_bytes=VMEM_LIMIT),
        cost_estimate=pl.CostEstimate(
            flops=micros * 1_100_000_000, bytes_accessed=3_000_000, transcendentals=0
        ),
    )(*args)


def share_order(y, core):
    f = jnp.arange(PAD)
    dp, row = f // 18, f % 18
    half = row // 9
    far = jnp.where((dp // 4 - y) % 2 == 0, 0, 144) + jnp.where(half == core, 0, SHARE)
    at = far + dp // 8 * 36 + dp % 4 * 9 + row % 9
    at = jnp.where(f < WIDTH, at, -1)
    return (at[:, None] == jnp.arange(PAD)[None, :]).astype(BF)


GROUPS_FAR = [[y * 4 + z for y in range(p, 8, 2) for z in range(4)] for p in range(2)]
SWAP = [(s, s ^ 1) for s in range(16)]


def spread(block, axis, groups):
    count = len(groups[0])
    return lax.all_to_all(
        jnp.broadcast_to(block[None], (count,) + block.shape), axis, 0, 0,
        axis_index_groups=groups, tiled=True,
    )


def along_z(distance):
    pairs = []
    for y in range(8):
        for z in range(4):
            for s in range(16):
                to = (z + (distance if s % 2 == 0 else -distance)) % 4
                pairs.append(((y * 4 + z) * 16 + s, (y * 4 + to) * 16 + s))
    return pairs


def along_y(distance):
    pairs = []
    for y in range(8):
        for z in range(4):
            for s in range(16):
                to = (y + (distance if s % 2 == 0 else -distance)) % 8
                pairs.append(((y * 4 + z) * 16 + s, (to * 4 + z) * 16 + s))
    return pairs


UP = along_y(1)


def move(a, pairs):
    return lax.ppermute(a, ("dp", "seq"), pairs)


def per_device(clips, qkv_spatial, out_spatial, qkv_temporal, out_temporal, cotangent):
    x = clips.reshape(TOKENS, D)
    out_grad = cotangent.reshape(TOKENS, D)
    seq, dp = lax.axis_index("seq"), lax.axis_index("dp")
    y, chip, core = dp // 4, seq // 2, seq % 2
    at = jnp.stack([y, core, chip, dp % 4]).astype(jnp.int32)

    tokens_b = ((TOKENS, D), BF)
    wide_b = ((TOKENS, 2 * D), BF)
    probs = (HEADS, TOKENS, TOKENS)
    sems = pltpu.SemaphoreType.DMA((16,))

    def turn(a):
        parts = a.reshape(16, PATCH_BLOCK, 2 * D)
        return lax.all_to_all(parts, "seq", 0, 0, tiled=True).reshape(TOKENS, 2 * D)

    packed, packed_h, packed_t, packed_th = call(
        pack_kernel, [((72, D), BF), ((36, D), BF)] * 2,
        [
            pltpu.VMEM((3, 36, WIDTH), BF), pltpu.VMEM((18, D), BF),
            pltpu.VMEM((3, 36, WIDTH), BF), pltpu.VMEM((18, D), BF), sems,
        ],
        2, at, qkv_spatial, out_spatial, qkv_temporal, out_temporal, hbm=range(1, 5),
    )

    def swap(a):
        return lax.ppermute(a, "seq", SWAP)

    def column(rows, near, far):
        return call(
            column_kernel, [((2 * BLOCK, D), BF)], [], 2,
            at, rows, near, far, swap(jnp.concatenate([near, far])),
        )[0]

    def onward(ring):
        ring.append(move(ring[-1], UP))
        theirs = swap(ring[-2])
        ring[-1], theirs = lax.optimization_barrier((ring[-1], theirs))
        return theirs

    def final(ring):
        theirs = swap(ring[3])
        last = move(lax.dynamic_slice_in_dim(ring[3], core * BLOCK, BLOCK, axis=0), UP)
        return lax.optimization_barrier((last, theirs))

    near, far = move(packed, along_z(1)), move(packed_h, along_z(2))
    near, far, packed_t, packed_th = lax.optimization_barrier((near, far, packed_t, packed_th))
    near_t, far_t = move(packed_t, along_z(1)), move(packed_th, along_z(2))
    wgrad_order = share_order(y, core)

    block = column(packed, near, far)
    ring = [block, move(block, UP)]
    ring[1], wgrad_order = lax.optimization_barrier((ring[1], wgrad_order))
    block_t = column(packed_t, near_t, far_t)
    theirs = [onward(ring)]
    ring[2], block_t = lax.optimization_barrier((ring[2], block_t))
    ring_t = [block_t, move(block_t, UP)]
    theirs.append(onward(ring))
    last, other = final(ring)
    ring_t.append(move(ring_t[-1], UP))
    last_other, ring_t[2] = lax.optimization_barrier((swap(last), ring_t[2]))
    blocks = [*ring, *theirs, other, last, last_other]
    ring_t.append(move(ring_t[-1], UP))
    theirs_t = [swap(ring_t[1]), swap(ring_t[2])]
    last_t, other = final(ring_t)
    blocks_t = [*ring_t, *theirs_t, other, last_t, swap(last_t)]

    more = pltpu.SemaphoreType.DMA((5,))
    weights = pltpu.VMEM((2 * D, D), BF)
    tokens, wide = pltpu.VMEM((TOKENS, D), BF), pltpu.VMEM((TOKENS, 2 * D), BF)
    kept = pltpu.VMEM((3, TOKENS, PAD), BF), pltpu.VMEM(probs, F32), pltpu.VMEM((TOKENS, PAD), BF)
    both, qkv, probs_s, context_s = call(
        forward_kernel,
        [wide_b, ((3, TOKENS, PAD), BF), (probs, F32), ((TOKENS, PAD), BF)],
        [weights, tokens, *kept, sems, more],
        8,
        at, x, out_grad, *blocks,
        hbm=range(1, 12), hbm_outs=(1, 2, 3),
    )
    both = turn(both)
    both_back, keep, send = call(
        temporal_kernel,
        [wide_b, ((SHARE, D), BF), ((SHARE, D), BF)],
        [weights, wide, pltpu.VMEM((PAD, PAD), BF), pltpu.VMEM(probs, F32), sems, more],
        12,
        at, both, wgrad_order, *blocks_t,
        hbm=range(1, 12),
    )
    both_back = turn(both_back)

    def add(a, b):
        return (a.astype(F32) + b.astype(F32)).astype(BF)

    total = add(keep, swap(send))
    total = add(total[:144], move(total[144:], UP))
    (input_grad,) = call(
        backward_kernel,
        [tokens_b],
        [weights, tokens, tokens, *kept, sems, more],
        9,
        at, x, both_back, qkv, probs_s, context_s, *blocks,
        hbm=range(1, 15),
    )
    over_z = lax.all_to_all(
        total.reshape(16, 9, D), "dp", 0, 0, axis_index_groups=GROUPS_FAR, tiled=True
    )
    over_z = jnp.sum(over_z.astype(F32), axis=0).astype(BF)
    over_z, input_grad = lax.optimization_barrier((over_z, input_grad))
    over_seq = spread(over_z, "seq", [list(range(16))]).reshape(8, 2, 9, D)
    out_temporal_grad = jnp.sum(over_seq.astype(F32), axis=0).reshape(18, D)
    mixed = both_back[:, D:]

    return mixed[None, None], input_grad[None, None], out_temporal_grad


def solution(mesh):
    tokens = P("dp", "seq", None, None)
    placed = (tokens, P(None, "dp", None), P("dp", None), P(None, "dp", None), P("dp", None), tokens)
    return jax.shard_map(
        per_device,
        mesh=mesh,
        in_specs=placed,
        out_specs=(tokens, tokens, P("dp", None)),
        check_vma=False,
    )
```

```python
import jax
import jax.numpy as jnp
from jax import lax
from jax.experimental import pallas as pl
from jax.experimental.pallas import tpu as pltpu
from jax.sharding import PartitionSpec as P

BF = jnp.bfloat16
F32 = jnp.float32
EPSILON = 1e-06
D = 1152
WIDTH = 576
PAD = 640
HEADS = 8
HEAD = 72
TOKENS = 128
PATCH_BLOCK = 8
SCALING = HEAD ** (-0.5)
SHARE = 288
BLOCK = 144
VMEM_LIMIT = 62 * 1024 * 1024


def nn(a, b):
    return lax.dot_general(a, b, (((1,), (0,)), ((), ())), preferred_element_type=F32)


def nt(a, b):
    return lax.dot_general(a, b, (((1,), (1,)), ((), ())), preferred_element_type=F32)


def tn(a, b):
    return lax.dot_general(a, b, (((0,), (0,)), ((), ())), preferred_element_type=F32)


def lanes(shape):
    return lax.broadcasted_iota(jnp.int32, shape, len(shape) - 1)


def normalize(values):
    centred = values - jnp.mean(values, axis=-1, keepdims=True)
    inverse = lax.rsqrt(jnp.mean(centred * centred, axis=-1, keepdims=True) + EPSILON)
    return centred * inverse, inverse


def norm_back(grad, normed, inverse):
    return inverse * (
        grad
        - jnp.mean(grad, axis=-1, keepdims=True)
        - normed * jnp.mean(grad * normed, axis=-1, keepdims=True)
    )


def keep_width(a):
    return jnp.where(lanes(a.shape) < WIDTH, a, 0.0)


def window(h):
    low = h * HEAD // 128 * 128
    high = -(-(h * HEAD + HEAD) // 128) * 128
    return low, high


def head_mask(h):
    low, high = window(h)
    at = lanes((TOKENS, high - low)) + low
    return (at >= h * HEAD) & (at < h * HEAD + HEAD)


def add_window(tiles, h, part):
    low, high = window(h)
    part = jnp.where(head_mask(h), part, 0.0)
    for t in range(low // 128, high // 128):
        piece = part[:, t * 128 - low : t * 128 - low + 128]
        tiles[t] = piece if tiles[t] is None else tiles[t] + piece


def join(tiles):
    return jnp.concatenate(tiles, axis=1)


def rounded(a):
    return a.astype(BF).astype(F32)


def attend(q, k, v, allowed, probs_ref):
    tiles = [None] * (PAD // 128)
    for h in range(HEADS):
        low, high = window(h)
        masked = jnp.where(head_mask(h), q[:, low:high].astype(F32), 0.0).astype(BF)
        scores = nt(masked, k[:, low:high]) * SCALING
        if allowed is not None:
            scores = jnp.where(allowed, scores, -1e38)
        powers = jnp.exp(scores - jnp.max(scores, axis=-1, keepdims=True))
        probs = powers / jnp.sum(powers, axis=-1, keepdims=True)
        probs_ref[h] = probs
        add_window(tiles, h, nn(probs.astype(BF), v[:, low:high]))
    return join(tiles).astype(BF)


def attend_back(q, k, v, context, context_grad, probs_ref):
    dq, dk, dv = ([None] * (PAD // 128) for _ in range(3))
    for h in range(HEADS):
        low, high = window(h)
        grad = context_grad[:, low:high]
        masked = jnp.where(head_mask(h), grad.astype(F32), 0.0)
        probs = probs_ref[h]
        prob_grad = nt(masked.astype(BF), v[:, low:high])
        row = jnp.sum(masked * context[:, low:high].astype(F32), axis=-1, keepdims=True)
        score_grad = (probs * (prob_grad - row) * SCALING).astype(BF)
        add_window(dv, h, tn(probs.astype(BF), grad))
        add_window(dq, h, nn(score_grad, k[:, low:high]))
        add_window(dk, h, tn(score_grad, q[:, low:high]))
    return rounded(join(dq)), rounded(join(dk)), rounded(join(dv))


def start_all(copies):
    for copy in copies:
        copy.start()
    return copies


def wait_all(copies):
    for copy in copies:
        copy.wait()


def load_weights(at_ref, blocks, weights, sems, order):
    y, core = at_ref[0], at_ref[1]
    sign = 1 - 2 * core

    def copy(source, half, place, sem):
        at = pl.multiple_of(half * D + lax.rem(place + 16, 8) * BLOCK, BLOCK)
        return pltpu.make_async_copy(source, weights.at[pl.ds(at, BLOCK), :], sems.at[sem])

    last = start_all([copy(blocks[7], core, y + 4, 0), copy(blocks[8], 1 - core, y + 4, 8)])
    groups = {}
    for half in order:
        rows = pl.ds(half * BLOCK, BLOCK)
        copies = [copy(blocks[0].at[rows, :], half, y, half * 8 + 1)]
        for step in range(1, 4):
            below, above = blocks[step].at[rows, :], blocks[3 + step].at[rows, :]
            copies.append(copy(below, half, y - sign * step, half * 8 + 2 * step))
            copies.append(copy(above, half, y + sign * step, half * 8 + 2 * step + 1))
        groups[half] = start_all(copies)
    groups[order[0]] = last + groups[order[0]]
    return groups


def project(normed, weights, wait_first, wait_second):
    normed_b = normed.astype(BF)
    wait_first()
    qk = nn(normed_b, weights[:D, :])
    wait_second()
    v = keep_width(nn(normed_b, weights[D:, :PAD]))
    k = pltpu.roll(qk, WIDTH, 1)
    return qk[:, :PAD].astype(BF), k[:, :PAD].astype(BF), v.astype(BF)


def pair_lanes(dq, dk):
    zeros = jnp.zeros((TOKENS, D - PAD), F32)
    return jnp.concatenate([dq, zeros], axis=1) + pltpu.roll(
        jnp.concatenate([dk, zeros], axis=1), WIDTH, 1
    )


def back_project(dq, dk, dv, weights):
    return nt(pair_lanes(dq, dk).astype(BF), weights[:D, :]) + nt(dv.astype(BF), weights[D:, :PAD])


def late(a):
    return jnp.where(lanes(a.shape) >= PAD - WIDTH, a, 0.0)


def out_weights(weights, side):
    starts = [D + y * BLOCK + side * 72 for y in range(8)]
    return jnp.concatenate([weights[at : at + 72, D - PAD :] for at in starts], axis=0)


def project_out(context, left, right):
    zeros = jnp.zeros((TOKENS, D - PAD), F32)
    context = context[:, :WIDTH]
    first, second = late(nn(context, left)), late(nn(context, right))
    return pltpu.roll(
        jnp.concatenate([first, zeros], axis=1), D - (PAD - WIDTH), 1
    ) + jnp.concatenate([zeros, second], axis=1)


def back_project_out(grad, left, right):
    first = late(pltpu.roll(grad, PAD - WIDTH, 1)[:, :PAD])
    second = late(grad[:, D - PAD :])
    context_grad = nt(first.astype(BF), left) + nt(second.astype(BF), right)
    return jnp.concatenate([context_grad, jnp.zeros((TOKENS, PAD - WIDTH), F32)], axis=1).astype(BF)


def selection(rows, columns, shift):
    r = lax.broadcasted_iota(jnp.int32, (rows, columns), 0)
    c = lax.broadcasted_iota(jnp.int32, (rows, columns), 1)
    return r + shift == c


def pack_kernel(at_ref, *refs):
    outside, inside_refs, sems = refs[:4], refs[8:12], refs[12]
    wait_all(
        start_all(
            [
                pltpu.make_async_copy(a, b, sems.at[n])
                for n, (a, b) in enumerate(zip(outside, inside_refs))
            ]
        )
    )
    qkv_s, out_s, qkv_t, out_t = inside_refs
    core = at_ref[1]

    def pick(which, a):
        return nn(which.astype(F32).astype(BF), a)

    def side(a, b):
        return jnp.concatenate([a, b], axis=1)

    lead = selection(36, 18, 0)
    tail = selection(36, 18, -18)

    def blocks(qkv, out_ref):
        q, k, v, out = qkv[0], qkv[1], qkv[2], out_ref[...]
        halves = pick(lead, out[:, :WIDTH]) + pick(tail, out[:, WIDTH:])
        return side(q.astype(F32), k.astype(F32)), side(v.astype(F32), halves)

    for n, (qkv, out_ref) in enumerate(((qkv_s, out_s), (qkv_t, out_t))):
        all_ref, half_ref = refs[4 + 2 * n : 6 + 2 * n]
        first, second = blocks(qkv, out_ref)
        half_ref[...] = jnp.where(core == 0, first, second).astype(BF)
        all_ref[...] = jnp.concatenate([first, second], axis=0).astype(BF)


def in_sides(parts):
    plain = jnp.concatenate(parts, axis=0)
    by_side = jnp.concatenate([p[:18] for p in parts] + [p[18:] for p in parts], axis=0)
    return jnp.where(lanes(plain.shape) < WIDTH, plain, by_side)


def in_order(z, own, below, above, far):
    parts = []
    for place in range(4):
        distance = lax.rem(place - z + 4, 4)
        part = jnp.where(distance == 0, own, jnp.where(distance == 1, above, far))
        parts.append(jnp.where(distance == 3, below, part))
    return parts


def column_kernel(at_ref, own_ref, next_ref, far_ref, other_ref, block_ref):
    z, core = at_ref[3], at_ref[1]
    own, near, far = (ref[...].astype(F32) for ref in (own_ref, next_ref, far_ref))
    other = other_ref[...].astype(F32)
    below = jnp.where(core == 0, near, other[:72])
    above = jnp.where(core == 0, other[:72], near)
    low = jnp.where(core == 0, far, other[72:])
    high = jnp.where(core == 0, other[72:], far)
    first = in_order(z, own[:36], below[:36], above[:36], low)
    second = in_order(z, own[36:], below[36:], above[36:], high)
    block_ref[:BLOCK] = jnp.concatenate(first, axis=0).astype(BF)
    block_ref[BLOCK:] = in_sides(second).astype(BF)


def fetch(pairs, sems):
    return start_all(
        [pltpu.make_async_copy(a, b, sems.at[n]) for n, (a, b) in enumerate(pairs)]
    )


def forward_kernel(at_ref, x_hbm, cot_hbm, *refs):
    blocks, refs = refs[:9], refs[9:]
    both_ref, *outside, weights, x_ref, qkv_ref, probs_ref, context_ref, sems, more = refs
    tokens = fetch([(x_hbm, x_ref)], more)
    groups = load_weights(at_ref, blocks, weights, sems, (0, 1))
    cotangent = pltpu.make_async_copy(cot_hbm, both_ref.at[:, pl.ds(D, D)], more.at[1])
    cotangent.start()
    wait_all(tokens)
    x = x_ref[...].astype(F32)
    q, k, v = project(
        normalize(x)[0], weights, lambda: wait_all(groups[0]), lambda: wait_all(groups[1])
    )
    qkv_ref[0], qkv_ref[1], qkv_ref[2] = q, k, v
    left, right = out_weights(weights, 0), out_weights(weights, 1)
    context = attend(q, k, v, None, probs_ref)
    context_ref[...] = context
    copies = fetch(zip((qkv_ref, probs_ref, context_ref), outside), sems)
    both_ref[:, :D] = (x + project_out(context, left, right)).astype(BF)
    cotangent.wait()
    wait_all(copies)


def temporal_kernel(at_ref, both_hbm, order_hbm, *refs):
    back_ref, keep_ref, send_ref, weights, both_ref, order_ref, probs, sems, more = refs[9:]
    tokens, order = fetch([(both_hbm, both_ref), (order_hbm, order_ref)], more)
    groups = load_weights(at_ref, refs[:9], weights, sems, (0, 1))
    tokens.wait()
    hidden = both_ref[:, :D].astype(F32)
    normed, inverse = normalize(hidden)
    q, k, v = project(
        normed, weights, lambda: wait_all(groups[0]), lambda: wait_all(groups[1])
    )
    left, right = out_weights(weights, 0), out_weights(weights, 1)
    rows = lax.broadcasted_iota(jnp.int32, (TOKENS, TOKENS), 0)
    cols = lax.broadcasted_iota(jnp.int32, (TOKENS, TOKENS), 1)
    allowed = (rows & (PATCH_BLOCK - 1)) == (cols & (PATCH_BLOCK - 1))
    context = attend(q, k, v, allowed, probs)
    cot = both_ref[:, D:]
    order.wait()
    share = tn(nn(context, order_ref[...]).astype(BF), cot).astype(BF)
    keep_ref[...], send_ref[...] = share[:SHARE], share[SHARE:WIDTH]
    back_ref[:, D:] = (hidden + project_out(context, left, right)).astype(BF)
    cot = cot.astype(F32)
    context_grad = back_project_out(cot, left, right)
    dq, dk, dv = attend_back(q, k, v, context, context_grad, probs)
    normed_grad = rounded(back_project(dq, dk, dv, weights))
    back_ref[:, :D] = (cot + norm_back(normed_grad, normed, inverse)).astype(BF)


def backward_kernel(at_ref, x_hbm, both_hbm, qkv_hbm, probs_hbm, context_hbm, *refs):
    blocks, refs = refs[:9], refs[9:]
    input_grad_ref, weights, x_ref, grad_ref, qkv_ref, probs_ref, context_ref, sems, more = refs
    copies = fetch([(both_hbm.at[:, pl.ds(0, D)], grad_ref), (x_hbm, x_ref)], more)
    groups = load_weights(at_ref, blocks, weights, sems, (1, 0))
    kept = (qkv_hbm, qkv_ref), (probs_hbm, probs_ref), (context_hbm, context_ref)
    copies += [pltpu.make_async_copy(a, b, more.at[2 + n]) for n, (a, b) in enumerate(kept)]
    start_all(copies[2:])
    wait_all(copies[:2])
    grad = grad_ref[...].astype(F32)
    normed, inverse = normalize(x_ref[...].astype(F32))
    wait_all(groups[1])
    context_grad = back_project_out(grad, out_weights(weights, 0), out_weights(weights, 1))
    wait_all(copies[2:])
    dq, dk, dv = attend_back(
        qkv_ref[0], qkv_ref[1], qkv_ref[2], context_ref[...], context_grad, probs_ref
    )
    wait_all(groups[0])
    normed_grad = back_project(dq, dk, dv, weights)
    input_grad_ref[...] = (grad + norm_back(normed_grad, normed, inverse)).astype(BF)


def call(kernel, outs, scratch, micros, *args, smem=True, hbm=(), hbm_outs=()):
    in_specs = []
    for at in range(len(args)):
        space = pltpu.VMEM
        if smem and at == 0:
            space = pltpu.SMEM
        elif at in hbm:
            space = pl.ANY
        in_specs.append(pl.BlockSpec(memory_space=space))
    return pl.pallas_call(
        kernel,
        out_shape=[jax.ShapeDtypeStruct(s, t) for s, t in outs],
        in_specs=in_specs,
        out_specs=[
            pl.BlockSpec(memory_space=pl.ANY if n in hbm_outs else pltpu.VMEM)
            for n in range(len(outs))
        ],
        scratch_shapes=scratch,
        compiler_params=pltpu.CompilerParams(vmem_limit_bytes=VMEM_LIMIT),
        cost_estimate=pl.CostEstimate(
            flops=micros * 1_100_000_000, bytes_accessed=3_000_000, transcendentals=0
        ),
    )(*args)


def share_order(y, core):
    f = jnp.arange(PAD)
    dp, row = f // 18, f % 18
    half = row // 9
    far = jnp.where((dp // 4 - y) % 2 == 0, 0, 144) + jnp.where(half == core, 0, SHARE)
    at = far + dp // 8 * 36 + dp % 4 * 9 + row % 9
    at = jnp.where(f < WIDTH, at, -1)
    return (at[:, None] == jnp.arange(PAD)[None, :]).astype(BF)


GROUPS_FAR = [[y * 4 + z for y in range(p, 8, 2) for z in range(4)] for p in range(2)]
SWAP = [(s, s ^ 1) for s in range(16)]


def spread(block, axis, groups):
    count = len(groups[0])
    return lax.all_to_all(
        jnp.broadcast_to(block[None], (count,) + block.shape), axis, 0, 0,
        axis_index_groups=groups, tiled=True,
    )


def along_z(distance):
    pairs = []
    for y in range(8):
        for z in range(4):
            for s in range(16):
                to = (z + (distance if s % 2 == 0 else -distance)) % 4
                pairs.append(((y * 4 + z) * 16 + s, (y * 4 + to) * 16 + s))
    return pairs


def along_y(distance):
    pairs = []
    for y in range(8):
        for z in range(4):
            for s in range(16):
                to = (y + (distance if s % 2 == 0 else -distance)) % 8
                pairs.append(((y * 4 + z) * 16 + s, (to * 4 + z) * 16 + s))
    return pairs


UP = along_y(1)


def move(a, pairs):
    return lax.ppermute(a, ("dp", "seq"), pairs)


def per_device(clips, qkv_spatial, out_spatial, qkv_temporal, out_temporal, cotangent):
    x = clips.reshape(TOKENS, D)
    out_grad = cotangent.reshape(TOKENS, D)
    seq, dp = lax.axis_index("seq"), lax.axis_index("dp")
    y, chip, core = dp // 4, seq // 2, seq % 2
    at = jnp.stack([y, core, chip, dp % 4]).astype(jnp.int32)

    tokens_b = ((TOKENS, D), BF)
    wide_b = ((TOKENS, 2 * D), BF)
    probs = (HEADS, TOKENS, TOKENS)
    sems = pltpu.SemaphoreType.DMA((16,))

    def turn(a):
        parts = a.reshape(16, PATCH_BLOCK, 2 * D)
        return lax.all_to_all(parts, "seq", 0, 0, tiled=True).reshape(TOKENS, 2 * D)

    packed, packed_h, packed_t, packed_th = call(
        pack_kernel, [((72, D), BF), ((36, D), BF)] * 2,
        [
            pltpu.VMEM((3, 36, WIDTH), BF), pltpu.VMEM((18, D), BF),
            pltpu.VMEM((3, 36, WIDTH), BF), pltpu.VMEM((18, D), BF), sems,
        ],
        2, at, qkv_spatial, out_spatial, qkv_temporal, out_temporal, hbm=range(1, 5),
    )

    def swap(a):
        return lax.ppermute(a, "seq", SWAP)

    def column(rows, near, far):
        return call(
            column_kernel, [((2 * BLOCK, D), BF)], [], 2,
            at, rows, near, far, swap(jnp.concatenate([near, far])),
        )[0]

    def onward(ring):
        ring.append(move(ring[-1], UP))
        theirs = swap(ring[-2])
        ring[-1], theirs = lax.optimization_barrier((ring[-1], theirs))
        return theirs

    def final(ring):
        theirs = swap(ring[3])
        last = move(lax.dynamic_slice_in_dim(ring[3], core * BLOCK, BLOCK, axis=0), UP)
        return lax.optimization_barrier((last, theirs))

    near, far = move(packed, along_z(1)), move(packed_h, along_z(2))
    near, far, packed_t, packed_th = lax.optimization_barrier((near, far, packed_t, packed_th))
    near_t, far_t = move(packed_t, along_z(1)), move(packed_th, along_z(2))
    wgrad_order = share_order(y, core)

    block = column(packed, near, far)
    ring = [block, move(block, UP)]
    ring[1], wgrad_order = lax.optimization_barrier((ring[1], wgrad_order))
    block_t = column(packed_t, near_t, far_t)
    theirs = [onward(ring)]
    ring[2], block_t = lax.optimization_barrier((ring[2], block_t))
    ring_t = [block_t, move(block_t, UP)]
    theirs.append(onward(ring))
    last, other = final(ring)
    ring_t.append(move(ring_t[-1], UP))
    last_other, ring_t[2] = lax.optimization_barrier((swap(last), ring_t[2]))
    blocks = [*ring, *theirs, other, last, last_other]
    ring_t.append(move(ring_t[-1], UP))
    piece = lax.dynamic_slice_in_dim(ring_t[3], core * BLOCK, BLOCK, axis=0)
    piece, *ring_t[1:] = lax.optimization_barrier((piece, *ring_t[1:]))
    last_t = move(piece, UP)
    blocks_t = [*ring_t, *map(swap, ring_t[1:]), last_t, swap(last_t)]

    more = pltpu.SemaphoreType.DMA((5,))
    weights = pltpu.VMEM((2 * D, D), BF)
    tokens, wide = pltpu.VMEM((TOKENS, D), BF), pltpu.VMEM((TOKENS, 2 * D), BF)
    kept = pltpu.VMEM((3, TOKENS, PAD), BF), pltpu.VMEM(probs, F32), pltpu.VMEM((TOKENS, PAD), BF)
    both, qkv, probs_s, context_s = call(
        forward_kernel,
        [wide_b, ((3, TOKENS, PAD), BF), (probs, F32), ((TOKENS, PAD), BF)],
        [weights, tokens, *kept, sems, more],
        8,
        at, x, out_grad, *blocks,
        hbm=range(1, 12), hbm_outs=(1, 2, 3),
    )
    both = turn(both)
    both_back, keep, send = call(
        temporal_kernel,
        [wide_b, ((SHARE, D), BF), ((SHARE, D), BF)],
        [weights, wide, pltpu.VMEM((PAD, PAD), BF), pltpu.VMEM(probs, F32), sems, more],
        12,
        at, both, wgrad_order, *blocks_t,
        hbm=range(1, 12),
    )
    both_back = turn(both_back)

    def add(a, b):
        return (a.astype(F32) + b.astype(F32)).astype(BF)

    total = add(keep, swap(send))
    total = add(total[:144], move(total[144:], UP))
    (input_grad,) = call(
        backward_kernel,
        [tokens_b],
        [weights, tokens, tokens, *kept, sems, more],
        9,
        at, x, both_back, qkv, probs_s, context_s, *blocks,
        hbm=range(1, 15),
    )
    over_z = lax.all_to_all(
        total.reshape(16, 9, D), "dp", 0, 0, axis_index_groups=GROUPS_FAR, tiled=True
    )
    over_z = jnp.sum(over_z.astype(F32), axis=0).astype(BF)
    over_z, input_grad = lax.optimization_barrier((over_z, input_grad))
    over_seq = spread(over_z, "seq", [list(range(16))]).reshape(8, 2, 9, D)
    out_temporal_grad = jnp.sum(over_seq.astype(F32), axis=0).reshape(18, D)
    mixed = both_back[:, D:]

    return mixed[None, None], input_grad[None, None], out_temporal_grad


def solution(mesh):
    tokens = P("dp", "seq", None, None)
    placed = (tokens, P(None, "dp", None), P("dp", None), P(None, "dp", None), P("dp", None), tokens)
    return jax.shard_map(
        per_device,
        mesh=mesh,
        in_specs=placed,
        out_specs=(tokens, tokens, P("dp", None)),
        check_vma=False,
    )
```
